512 devices in a mesh: clip: 2 (over core), tower: 2 (over z_lo), seq: 128 (over x, y, z_hi).
Axes of the slice: x: 4, y: 8, z: 8 (z_hi: 4, z_lo: 2; z = z_hi * 2 + z_lo), core: 2. Of those that a mesh axis runs over, the one named last changes fastest.
Arguments:
- video_query: bfloat16 [65536, 1536], P(('clip', 'tower', 'seq')), parts along dimension 0, may hold values from -4.5 to 4.5
- video_keys: bfloat16 [65536, 1536], P(('clip', 'tower', 'seq')), parts along dimension 0, may hold values from -4.5 to 4.5
- video_value: bfloat16 [65536, 1536], P(('clip', 'tower', 'seq')), parts along dimension 0, may hold values from -6 to 6
- audio_query: bfloat16 [32768, 1536], P(('clip', 'tower', 'seq')), parts along dimension 0, may hold values from -4.5 to 4.5
- audio_key: bfloat16 [32768, 1536], P(('clip', 'tower', 'seq')), parts along dimension 0, may hold values from -4.5 to 4.5
- audio_value: bfloat16 [32768, 1536], P(('clip', 'tower', 'seq')), parts along dimension 0, may hold values from -6 to 6
- video_cotangent: bfloat16 [65536, 1536], P(('clip', 'tower', 'seq')), parts along dimension 0, may hold values from -6 to 6
- audio_cotangent: bfloat16 [32768, 1536], P(('clip', 'tower', 'seq')), parts along dimension 0, may hold values from -6 to 6
- video_lists: int32 [512, 2], P(('clip', 'tower', 'seq')), parts along dimension 0, may hold values from 0 to 255, as said below
- audio_lists: int32 [512, 2], P(('clip', 'tower', 'seq')), parts along dimension 0, may hold values from 0 to 255, as said below
Outputs:
- video_output: bfloat16 [65536, 1536], P(('clip', 'tower', 'seq')), parts along dimension 0
- audio_output: bfloat16 [32768, 1536], P(('clip', 'tower', 'seq')), parts along dimension 0
- video_query_grad: bfloat16 [65536, 1536], P(('clip', 'tower', 'seq')), parts along dimension 0
- video_key_grad: bfloat16 [65536, 1536], P(('clip', 'tower', 'seq')), parts along dimension 0
- video_value_grad: bfloat16 [65536, 1536], P(('clip', 'tower', 'seq')), parts along dimension 0
- audio_query_grad: bfloat16 [32768, 1536], P(('clip', 'tower', 'seq')), parts along dimension 0
- audio_key_grad: bfloat16 [32768, 1536], P(('clip', 'tower', 'seq')), parts along dimension 0
- audio_value_grad: bfloat16 [32768, 1536], P(('clip', 'tower', 'seq')), parts along dimension 0
The draws below stay inside these ranges and needn't reach their ends.
There are 2 independent parts, one for each index of `clip`. The reference program is written for one: setup_inputs(seed, part) draws one part's arguments, and reference() takes and returns one part's arrays. A program takes and returns all parts, laid end to end along the dimension named above; each array names one. Nothing has to cross between parts.
Inputs may be any that keep to these rules, and one draw needn't show every extreme that they name: `video_lists`: row b holds 2 consecutive block numbers, the first between max(b - 2, 0) and min(b, 254). `audio_lists`: row b holds 2 consecutive block numbers, the first between max(b - 2, 0) and min(b, 254).
All inputs are finite; a program needn't handle non-finite values.
Results may differ from the reference program's by a relative error of at most 0.012.
Values may be sent and summed in bfloat16 or wider, within the bound.
No kernel may reach another device: no remote copies, remote signals or barrier semaphores. Data moves between devices by JAX's collectives and lax.ppermute only.
A program may use at most 64 MiB of HBM per device.

```python
import jax
import jax.numpy as jnp
from jax import lax

HEADS = 12
HEAD_SIZE = 128
VIDEO_BLOCK_SIZE = 128
AT_DEV = 64
WINDOW_BLOCKS = 4
HALF_WINDOW = 2
LIST = 2
BLOCKS = 256
WIDTH = 1536
VIDEO_TOKENS = 32768
AUDIO_TOKENS = 16384
N_TOWER = 2
N_SEQ = 128


def normal_field(key, rows):
    return jnp.clip(jax.random.normal(key, (rows, WIDTH), jnp.float32), -4.5, 4.5)


def block_lists(key):
    block_ids = jnp.arange(BLOCKS, dtype=jnp.int32)
    jitter = jax.random.randint(key, (BLOCKS,), -HALF_WINDOW, 1, dtype=jnp.int32)
    starts = jnp.clip(block_ids + jitter, 0, BLOCKS - LIST)
    starts = jnp.where(block_ids == BLOCKS - 1, BLOCKS - LIST, starts)
    return (starts[:, None] + jnp.arange(LIST, dtype=jnp.int32)[None, :]).astype(jnp.int32)


def draw_video_query(key, part):
    key = jax.random.fold_in(key, 1)
    return normal_field(key, VIDEO_TOKENS).astype(jnp.bfloat16)


def draw_video_keys(key, part):
    key = jax.random.fold_in(key, 2)
    return normal_field(key, VIDEO_TOKENS).astype(jnp.bfloat16)


def draw_audio_query(key, part):
    key = jax.random.fold_in(key, 3)
    return normal_field(key, AUDIO_TOKENS).astype(jnp.bfloat16)


def draw_audio_key(key, part):
    key = jax.random.fold_in(key, 4)
    return normal_field(key, AUDIO_TOKENS).astype(jnp.bfloat16)


def draw_video_lists(key, part):
    key = jax.random.fold_in(key, 7)
    return block_lists(key)


def draw_audio_lists(key, part):
    key = jax.random.fold_in(key, 8)
    return block_lists(key)


def block_levels(key, shape, pieces, least, top_value):
    loudness = 1.0
    for position, blocks in pieces:
        heights = jax.random.uniform(jax.random.fold_in(jax.random.fold_in(key, 6), position), (blocks,), jnp.float32, least / len(pieces), top_value / len(pieces))
        loudness = loudness * jnp.repeat(jnp.exp(heights), shape[position] // blocks).reshape((-1,) + (1,) * (len(shape) - 1 - position))
    return loudness


def scatter_about(stream_key, extent, scale, limit, split=(), kind=jnp.bfloat16):
    values = scale * jax.random.normal(stream_key, extent, jnp.float32)
    if split:
        values = values * block_levels(stream_key, extent, split, -0.22, 0.18)
    return jnp.clip(values, -limit, limit).astype(kind)


def setup_inputs(seed: int = 0, part: int = 0) -> dict:
    streams_of = jax.random.split(jax.random.key(seed), 11)
    own_keys = jax.random.split(jax.random.fold_in(streams_of[10], part), 11)
    video_query = draw_video_query(jax.random.fold_in(jax.random.fold_in(streams_of[10], part), 71), part)
    video_keys = draw_video_keys(jax.random.fold_in(jax.random.fold_in(streams_of[10], part), 71), part)
    video_value = scatter_about(own_keys[2], (VIDEO_TOKENS, WIDTH), 1.0, 6.0, ((0, 256),))
    audio_query = draw_audio_query(jax.random.fold_in(jax.random.fold_in(streams_of[10], part), 71), part)
    audio_key = draw_audio_key(jax.random.fold_in(jax.random.fold_in(streams_of[10], part), 71), part)
    audio_value = scatter_about(own_keys[5], (AUDIO_TOKENS, WIDTH), 1.0, 6.0, ((0, 256),))
    video_cotangent = scatter_about(own_keys[6], (VIDEO_TOKENS, WIDTH), 1.0, 6.0, ((0, 256),))
    audio_cotangent = scatter_about(own_keys[7], (AUDIO_TOKENS, WIDTH), 1.0, 6.0, ((0, 256),))
    video_lists = draw_video_lists(jax.random.fold_in(jax.random.fold_in(streams_of[10], part), 71), part)
    audio_lists = draw_audio_lists(jax.random.fold_in(jax.random.fold_in(streams_of[10], part), 71), part)
    return {"video_query": video_query, "video_keys": video_keys, "video_value": video_value, "audio_query": audio_query, "audio_key": audio_key, "audio_value": audio_value, "video_cotangent": video_cotangent, "audio_cotangent": audio_cotangent, "video_lists": video_lists, "audio_lists": audio_lists}


HIGH_PRECISION = lax.Precision.HIGHEST


def attend_forward(queries, key_rows, value_rows, keep_mask):
    query_row_block = queries.shape[0]
    key_row_block = key_rows.shape[0]
    heads_query = queries.astype(jnp.float32).reshape(query_row_block, HEADS, HEAD_SIZE)
    heads_key = key_rows.astype(jnp.float32).reshape(key_row_block, HEADS, HEAD_SIZE)
    heads_value = value_rows.astype(jnp.float32).reshape(key_row_block, HEADS, HEAD_SIZE)
    score_matrix = jnp.einsum("xfk,ifk->fxi", heads_query, heads_key, precision=HIGH_PRECISION) * (HEAD_SIZE ** -0.5)
    score_matrix = jnp.where(keep_mask[None, None, :], score_matrix, -1e30)
    row_max = jnp.max(score_matrix, axis=-1, keepdims=True)
    weights = jnp.exp(score_matrix - row_max)
    weights = weights / jnp.sum(weights, axis=-1, keepdims=True)
    rounded_values = lax.optimization_barrier(weights.astype(jnp.bfloat16)).astype(jnp.float32)
    final_output = jnp.einsum("uwx,xue->wue", rounded_values, heads_value, precision=HIGH_PRECISION)
    return final_output, weights, rounded_values


def attend_backward(queries, key_rows, value_rows, cotangent, final_output, weights, rounded_values):
    query_row_block = queries.shape[0]
    key_row_block = key_rows.shape[0]
    heads_query = queries.astype(jnp.float32).reshape(query_row_block, HEADS, HEAD_SIZE)
    heads_key = key_rows.astype(jnp.float32).reshape(key_row_block, HEADS, HEAD_SIZE)
    heads_value = value_rows.astype(jnp.float32).reshape(key_row_block, HEADS, HEAD_SIZE)
    cotangent_heads = cotangent.astype(jnp.float32).reshape(query_row_block, HEADS, HEAD_SIZE)
    weight_gradient = jnp.einsum("xfk,ifk->fxi", cotangent_heads, heads_value, precision=HIGH_PRECISION)
    row_dots = jnp.sum(cotangent_heads * final_output, axis=-1).T
    grad_scores = weights * (weight_gradient - row_dots[:, :, None]) * (HEAD_SIZE ** -0.5)
    gradient_rounded = lax.optimization_barrier(grad_scores.astype(jnp.bfloat16)).astype(jnp.float32)
    query_term = jnp.einsum("uwx,xue->wue", gradient_rounded, heads_key, precision=HIGH_PRECISION).reshape(query_row_block, -1)
    key_term = jnp.einsum("sxj,xsw->jsw", gradient_rounded, heads_query, precision=HIGH_PRECISION).reshape(key_row_block, -1)
    value_term = jnp.einsum("sxj,xsw->jsw", rounded_values, cotangent_heads, precision=HIGH_PRECISION).reshape(key_row_block, -1)
    return query_term, key_term, value_term


def listed_mask(block_index, lists_row, rows):
    slots = block_index - HALF_WINDOW + jnp.arange(WINDOW_BLOCKS, dtype=jnp.int32)
    listed = jnp.any(lists_row[None, :] == slots[:, None], axis=1)
    return jnp.broadcast_to(listed[:, None], (WINDOW_BLOCKS, rows)).reshape(WINDOW_BLOCKS * rows)


def inside_mask(block_index, count, rows):
    slots = block_index - HALF_WINDOW + jnp.arange(WINDOW_BLOCKS, dtype=jnp.int32)
    inside = (slots >= 0) & (slots < count)
    return jnp.broadcast_to(inside[:, None], (WINDOW_BLOCKS, rows)).reshape(WINDOW_BLOCKS * rows)


def rounded_shared(values):
    return lax.optimization_barrier(values.astype(jnp.bfloat16)).astype(jnp.float32)


def reference(video_query, video_keys, video_value, audio_query, audio_key, audio_value, video_cotangent, audio_cotangent, video_lists, audio_lists):
    block_count = N_TOWER * N_SEQ
    window_width = video_query.shape[1]
    trailing = WINDOW_BLOCKS - HALF_WINDOW - 1

    def padded_input(array, rows):
        before = jnp.zeros((HALF_WINDOW * rows, window_width), array.dtype)
        after = jnp.zeros((trailing * rows, window_width), array.dtype)
        return jnp.concatenate([before, array, after], axis=0)

    padded_video_key = padded_input(video_keys, VIDEO_BLOCK_SIZE)
    pad_vvalue = padded_input(video_value, VIDEO_BLOCK_SIZE)
    pad_akey = padded_input(audio_key, AT_DEV)
    pad_avalue = padded_input(audio_value, AT_DEV)
    video_total = (block_count + WINDOW_BLOCKS - 1) * VIDEO_BLOCK_SIZE
    audio_total = (block_count + WINDOW_BLOCKS - 1) * AT_DEV
    initial = (jnp.zeros((video_total, window_width), jnp.float32), jnp.zeros((video_total, window_width), jnp.float32),
               jnp.zeros((audio_total, window_width), jnp.float32), jnp.zeros((audio_total, window_width), jnp.float32))

    def accumulate_block(total, share, start):
        current = lax.dynamic_slice_in_dim(total, start, share.shape[0], 0)
        return lax.dynamic_update_slice_in_dim(total, current + share, start, 0)

    def step(loop_carry, block_index):
        video_key_gradient, video_value_gradient, audio_key_gradient, audio_value_gradient = loop_carry
        video_begin_index = block_index * VIDEO_BLOCK_SIZE
        audio_start = block_index * AT_DEV
        window_keys = lax.dynamic_slice_in_dim(padded_video_key, video_begin_index, WINDOW_BLOCKS * VIDEO_BLOCK_SIZE, 0)
        value_window = lax.dynamic_slice_in_dim(pad_vvalue, video_begin_index, WINDOW_BLOCKS * VIDEO_BLOCK_SIZE, 0)
        akey_window = lax.dynamic_slice_in_dim(pad_akey, audio_start, WINDOW_BLOCKS * AT_DEV, 0)
        avalue_window = lax.dynamic_slice_in_dim(pad_avalue, audio_start, WINDOW_BLOCKS * AT_DEV, 0)
        own_query = lax.dynamic_slice_in_dim(video_query, video_begin_index, VIDEO_BLOCK_SIZE, 0)
        own_cot = lax.dynamic_slice_in_dim(video_cotangent, video_begin_index, VIDEO_BLOCK_SIZE, 0)
        aud_query = lax.dynamic_slice_in_dim(audio_query, audio_start, AT_DEV, 0)
        aud_cot = lax.dynamic_slice_in_dim(audio_cotangent, audio_start, AT_DEV, 0)
        self_keep = inside_mask(block_index, block_count, VIDEO_BLOCK_SIZE)
        cross_keep = listed_mask(block_index, video_lists[block_index], AT_DEV)
        audio_keep = listed_mask(block_index, audio_lists[block_index], VIDEO_BLOCK_SIZE)
        self_res, self_weights, self_rounded = attend_forward(own_query, window_keys, value_window, self_keep)
        cross_res, cross_weights, cross_rounded = attend_forward(own_query, akey_window, avalue_window, cross_keep)
        audio_res, audio_weights, audio_rounded = attend_forward(aud_query, window_keys, value_window, audio_keep)
        video_final_output = (self_res + cross_res).reshape(VIDEO_BLOCK_SIZE, window_width).astype(jnp.bfloat16)
        audio_final_output = audio_res.reshape(AT_DEV, window_width).astype(jnp.bfloat16)
        self_q, self_key_rows, self_v = attend_backward(own_query, window_keys, value_window, own_cot, self_res, self_weights, self_rounded)
        cross_q, cross_k, cross_v = attend_backward(own_query, akey_window, avalue_window, own_cot, cross_res, cross_weights, cross_rounded)
        audio_q, audio_key_rows, audio_v = attend_backward(aud_query, window_keys, value_window, aud_cot, audio_res, audio_weights, audio_rounded)
        video_query_gradient = (self_q + cross_q).astype(jnp.bfloat16)
        audio_query_gradient = audio_q.astype(jnp.bfloat16)
        video_key_gradient = accumulate_block(video_key_gradient, rounded_shared(self_key_rows + audio_key_rows), video_begin_index)
        video_value_gradient = accumulate_block(video_value_gradient, rounded_shared(self_v + audio_v), video_begin_index)
        audio_key_gradient = accumulate_block(audio_key_gradient, rounded_shared(cross_k), audio_start)
        audio_value_gradient = accumulate_block(audio_value_gradient, rounded_shared(cross_v), audio_start)
        return (video_key_gradient, video_value_gradient, audio_key_gradient, audio_value_gradient), (video_final_output, audio_final_output, video_query_gradient, audio_query_gradient)

    loop_carry, stacked = lax.scan(step, initial, jnp.arange(block_count, dtype=jnp.int32))
    video_output = stacked[0].reshape(-1, window_width)
    audio_output = stacked[1].reshape(-1, window_width)
    video_query_grad = stacked[2].reshape(-1, window_width)
    audio_query_grad = stacked[3].reshape(-1, window_width)
    video_begin = HALF_WINDOW * VIDEO_BLOCK_SIZE
    audio_begin = HALF_WINDOW * AT_DEV
    video_key_grad = loop_carry[0][video_begin:video_begin + block_count * VIDEO_BLOCK_SIZE].astype(jnp.bfloat16)
    video_value_grad = loop_carry[1][video_begin:video_begin + block_count * VIDEO_BLOCK_SIZE].astype(jnp.bfloat16)
    audio_key_grad = loop_carry[2][audio_begin:audio_begin + block_count * AT_DEV].astype(jnp.bfloat16)
    audio_value_grad = loop_carry[3][audio_begin:audio_begin + block_count * AT_DEV].astype(jnp.bfloat16)
    return (video_output, audio_output, video_query_grad, video_key_grad, video_value_grad,
            audio_query_grad, audio_key_grad, audio_value_grad)
```

```python
import functools

import jax
import jax.numpy as jnp
from jax import lax
from jax.experimental import pallas as pl
from jax.experimental.pallas import tpu as pltpu
from jax.sharding import Mesh
from jax.sharding import PartitionSpec as P

HEADS = 12
HEAD_SIZE = 128
WINDOW_BLOCKS = 4
HALF_WINDOW = 2
MEMBERS = 4
GROUP_HEADS = HEADS // MEMBERS
GROUP_WIDTH = GROUP_HEADS * HEAD_SIZE
EXTENDED = MEMBERS + WINDOW_BLOCKS - 1
VIDEO = 128
AUDIO = 64
STACK = VIDEO + AUDIO
ROWS = 2 * STACK
LIST_ROWS = 16
SCALE = HEAD_SIZE ** -0.5
LOG2_SCALE = SCALE * 1.4426950408889634
MASKED = -1e30
PARAMS = pltpu.CompilerParams(vmem_limit_bytes=40 * 1024 * 1024)


def product(left, right, left_dim, right_dim):
    return lax.dot_general(
        left,
        right,
        (((left_dim,), (right_dim,)), ((), ())),
        preferred_element_type=jnp.float32,
    )


def pack_kernel(
    video_list, audio_list, vq, vk, vv, aq, ak, av, vg, ag, kv_out, qg_out
):
    video_first = jnp.full((8, GROUP_WIDTH), video_list[0, 0].astype(jnp.float32))
    audio_first = jnp.full((8, GROUP_WIDTH), audio_list[0, 0].astype(jnp.float32))
    firsts = jnp.concatenate([video_first, audio_first], axis=0).astype(jnp.bfloat16)
    for member in range(MEMBERS):
        columns = slice(member * GROUP_WIDTH, (member + 1) * GROUP_WIDTH)
        kv_out[member, 0:128] = vk[:, columns]
        kv_out[member, 128:256] = vv[:, columns]
        kv_out[member, 256:320] = ak[:, columns]
        kv_out[member, 320:384] = av[:, columns]
        qg_out[member, 0:128] = vq[:, columns]
        qg_out[member, 128:192] = aq[:, columns]
        qg_out[member, 192:320] = vg[:, columns]
        qg_out[member, 320:384] = ag[:, columns]
        qg_out[member, 384:400] = firsts


def unpack_kernel(kv, qg, vo, ao, vqg, vkg, vvg, aqg, akg, avg):
    for member in range(MEMBERS):
        columns = slice(member * GROUP_WIDTH, (member + 1) * GROUP_WIDTH)
        vkg[:, columns] = kv[member, 0:128]
        vvg[:, columns] = kv[member, 128:256]
        akg[:, columns] = kv[member, 256:320]
        avg[:, columns] = kv[member, 320:384]
        vo[:, columns] = qg[member, 0:128]
        ao[:, columns] = qg[member, 128:192]
        vqg[:, columns] = qg[member, 192:320]
        aqg[:, columns] = qg[member, 320:384]


def merge_kernel(own, from_after, from_before, out):
    out[0] = (own[0] + from_before[...].astype(jnp.float32)).astype(jnp.bfloat16)
    out[1] = own[1].astype(jnp.bfloat16)
    out[2] = (own[2] + from_after[0].astype(jnp.float32)).astype(jnp.bfloat16)
    out[3] = (own[3] + from_after[1].astype(jnp.float32)).astype(jnp.bfloat16)


def weights_of(scaled):
    top = jnp.max(scaled, axis=1, keepdims=True)
    powers = jnp.exp2(scaled - top)
    return powers * (1.0 / jnp.sum(powers, axis=1, keepdims=True))


def attention_kernel(
    last_group,
    group_ref,
    kv,
    qg,
    before,
    after,
    qg_out,
    kv_out,
    before_out,
    after_out,
    vk,
    vv,
    ak,
    av,
    vk_sum,
    vv_sum,
    ak_sum,
    av_sum,
):
    group = group_ref[0]
    for block in range(EXTENDED):
        if block < HALF_WINDOW:
            source = before.at[block]
        elif block < HALF_WINDOW + MEMBERS:
            source = kv.at[block - HALF_WINDOW]
        else:
            source = after
        vk[block * VIDEO : (block + 1) * VIDEO] = source[0:128]
        vv[block * VIDEO : (block + 1) * VIDEO] = source[128:256]
        ak[block * AUDIO : (block + 1) * AUDIO] = source[256:320]
        av[block * AUDIO : (block + 1) * AUDIO] = source[320:384]
    vk_sum[...] = jnp.zeros_like(vk_sum)
    vv_sum[...] = jnp.zeros_like(vv_sum)
    ak_sum[...] = jnp.zeros_like(ak_sum)
    av_sum[...] = jnp.zeros_like(av_sum)
    bias_before = jnp.where(group == 0, MASKED, 0.0)
    bias_after = jnp.where(group == last_group, MASKED, 0.0)

    for member in range(MEMBERS):
        window_start = group * MEMBERS + member - HALF_WINDOW
        firsts = qg[member, ROWS : ROWS + LIST_ROWS].astype(jnp.float32)
        video_slot = jnp.max(firsts[0:8]).astype(jnp.int32) - window_start
        audio_slot = jnp.max(firsts[8:16]).astype(jnp.int32) - window_start
        queries = qg[member, 0:STACK]
        cotangents = qg[member, STACK:ROWS]
        window = slice(member * VIDEO, (member + WINDOW_BLOCKS) * VIDEO)
        keys = vk[window]
        values = vv[window]

        scaled = product(queries, keys, 1, 1) * LOG2_SCALE
        video_parts, audio_parts = [], []
        for slot in range(WINDOW_BLOCKS):
            block = member + slot
            part = scaled[:, slot * VIDEO : (slot + 1) * VIDEO]
            video_part = part[0:VIDEO]
            if block < HALF_WINDOW:
                video_part = video_part + bias_before
            elif block >= HALF_WINDOW + MEMBERS:
                video_part = video_part + bias_after
            listed = (audio_slot == slot) | (audio_slot + 1 == slot)
            video_parts.append(video_part)
            audio_parts.append(part[VIDEO:STACK] + jnp.where(listed, 0.0, MASKED))
        weights = jnp.concatenate(
            [
                weights_of(jnp.concatenate(video_parts, axis=1)),
                weights_of(jnp.concatenate(audio_parts, axis=1)),
            ],
            axis=0,
        )
        rounded = weights.astype(jnp.bfloat16)
        result = product(rounded, values, 1, 0)
        row_dot = jnp.sum(cotangents.astype(jnp.float32) * result, axis=1, keepdims=True)
        weight_grad = product(cotangents, values, 1, 1)
        score_grad = (weights * (weight_grad - row_dot)).astype(jnp.bfloat16)
        query_term = product(score_grad, keys, 1, 0)
        vk_sum[window] += product(score_grad, queries, 0, 0)
        vv_sum[window] += product(rounded, cotangents, 0, 0)

        listed_rows = pl.ds(pl.multiple_of((member + video_slot) * AUDIO, AUDIO), 2 * AUDIO)
        cross_keys = ak[listed_rows]
        cross_values = av[listed_rows]
        video_queries = queries[0:VIDEO]
        video_cotangents = cotangents[0:VIDEO]
        cross_weights = weights_of(product(video_queries, cross_keys, 1, 1) * LOG2_SCALE)
        cross_rounded = cross_weights.astype(jnp.bfloat16)
        cross_result = product(cross_rounded, cross_values, 1, 0)
        cross_dot = jnp.sum(
            video_cotangents.astype(jnp.float32) * cross_result, axis=1, keepdims=True
        )
        cross_grad = product(video_cotangents, cross_values, 1, 1)
        cross_score_grad = (cross_weights * (cross_grad - cross_dot)).astype(jnp.bfloat16)
        cross_query_term = product(cross_score_grad, cross_keys, 1, 0)
        ak_sum[listed_rows] += product(cross_score_grad, video_queries, 0, 0)
        av_sum[listed_rows] += product(cross_rounded, video_cotangents, 0, 0)

        qg_out[member, 0:128] = (result[0:VIDEO] + cross_result).astype(jnp.bfloat16)
        qg_out[member, 128:192] = result[VIDEO:STACK].astype(jnp.bfloat16)
        qg_out[member, 192:320] = (
            (query_term[0:VIDEO] + cross_query_term) * SCALE
        ).astype(jnp.bfloat16)
        qg_out[member, 320:384] = (query_term[VIDEO:STACK] * SCALE).astype(jnp.bfloat16)

    for block in range(EXTENDED):
        if block < HALF_WINDOW:
            target = before_out.at[block]
        elif block < HALF_WINDOW + MEMBERS:
            target = kv_out.at[block - HALF_WINDOW]
        else:
            target = after_out
        video_rows = slice(block * VIDEO, (block + 1) * VIDEO)
        audio_rows = slice(block * AUDIO, (block + 1) * AUDIO)
        target[0:128] = (vk_sum[video_rows] * SCALE).astype(target.dtype)
        target[128:256] = vv_sum[video_rows].astype(target.dtype)
        target[256:320] = (ak_sum[audio_rows] * SCALE).astype(target.dtype)
        target[320:384] = av_sum[audio_rows].astype(target.dtype)


def whole(memory=pltpu.VMEM):
    return pl.BlockSpec(memory_space=memory)


def pack(video_lists, audio_lists, *arrays):
    return pl.pallas_call(
        pack_kernel,
        out_shape=(
            jax.ShapeDtypeStruct((MEMBERS, ROWS, GROUP_WIDTH), jnp.bfloat16),
            jax.ShapeDtypeStruct((MEMBERS, ROWS + LIST_ROWS, GROUP_WIDTH), jnp.bfloat16),
        ),
        in_specs=[whole(pltpu.SMEM)] * 2 + [whole()] * 8,
        out_specs=(whole(), whole()),
        compiler_params=PARAMS,
        name="pack",
    )(video_lists, audio_lists, *arrays)


def unpack(kv, qg):
    video = jax.ShapeDtypeStruct((VIDEO, HEADS * HEAD_SIZE), jnp.bfloat16)
    audio = jax.ShapeDtypeStruct((AUDIO, HEADS * HEAD_SIZE), jnp.bfloat16)
    shapes = (video, audio, video, video, video, audio, audio, audio)
    return pl.pallas_call(
        unpack_kernel,
        out_shape=shapes,
        in_specs=[whole()] * 2,
        out_specs=[whole()] * 8,
        compiler_params=PARAMS,
        name="unpack",
    )(kv, qg)


def merge(own, from_after, from_before):
    return pl.pallas_call(
        merge_kernel,
        out_shape=jax.ShapeDtypeStruct(own.shape, jnp.bfloat16),
        in_specs=[whole()] * 3,
        out_specs=whole(),
        compiler_params=PARAMS,
        name="merge",
    )(own, from_after, from_before)


def attention(groups, group, kv, qg, before, after):
    def head_block(*leading):
        zeros = (0,) * len(leading)
        return pl.BlockSpec(leading + (HEAD_SIZE,), lambda head: zeros + (head,))

    video_sum = pltpu.VMEM((EXTENDED * VIDEO, HEAD_SIZE), jnp.float32)
    audio_sum = pltpu.VMEM((EXTENDED * AUDIO, HEAD_SIZE), jnp.float32)
    video_rows = pltpu.VMEM((EXTENDED * VIDEO, HEAD_SIZE), jnp.bfloat16)
    audio_rows = pltpu.VMEM((EXTENDED * AUDIO, HEAD_SIZE), jnp.bfloat16)
    return pl.pallas_call(
        functools.partial(attention_kernel, groups - 1),
        grid=(GROUP_HEADS,),
        out_shape=(
            jax.ShapeDtypeStruct((MEMBERS, ROWS, GROUP_WIDTH), jnp.bfloat16),
            jax.ShapeDtypeStruct((MEMBERS, ROWS, GROUP_WIDTH), jnp.float32),
            jax.ShapeDtypeStruct((HALF_WINDOW, ROWS, GROUP_WIDTH), jnp.bfloat16),
            jax.ShapeDtypeStruct((ROWS, GROUP_WIDTH), jnp.bfloat16),
        ),
        in_specs=[
            whole(pltpu.SMEM),
            head_block(MEMBERS, ROWS),
            head_block(MEMBERS, ROWS + LIST_ROWS),
            head_block(HALF_WINDOW, ROWS),
            head_block(ROWS),
        ],
        out_specs=(
            head_block(MEMBERS, ROWS),
            head_block(MEMBERS, ROWS),
            head_block(HALF_WINDOW, ROWS),
            head_block(ROWS),
        ),
        scratch_shapes=[video_rows] * 2 + [audio_rows] * 2 + [video_sum] * 2 + [audio_sum] * 2,
        compiler_params=PARAMS,
        name="attention",
    )(group, kv, qg, before, after)


def to_group(block, groups, distance):
    route = [(i, i + distance) for i in range(groups) if 0 <= i + distance < groups]
    return lax.ppermute(block, ("tower", "group"), route)


def exchange(packed):
    return lax.all_to_all(packed, "member", 0, 0)


def body(
    video_query,
    video_keys,
    video_value,
    audio_query,
    audio_key,
    audio_value,
    video_cotangent,
    audio_cotangent,
    video_lists,
    audio_lists,
):
    groups = lax.axis_size(("tower", "group"))
    group = lax.axis_index(("tower", "group")).astype(jnp.int32).reshape(1)
    kv_packed, qg_packed = pack(
        video_lists,
        audio_lists,
        video_query,
        video_keys,
        video_value,
        audio_query,
        audio_key,
        audio_value,
        video_cotangent,
        audio_cotangent,
    )
    kv = exchange(kv_packed)
    before = to_group(kv[MEMBERS - HALF_WINDOW :], groups, 1)
    after = to_group(kv[0], groups, -1)
    qg = exchange(qg_packed)
    qg_part, kv_part, before_part, after_part = attention(
        groups, group, kv, qg, before, after
    )
    from_after = to_group(before_part, groups, -1)
    from_before = to_group(after_part, groups, 1)
    qg_back = exchange(qg_part)
    kv_back = exchange(merge(kv_part, from_after, from_before))
    return unpack(kv_back, qg_back)


def solution(mesh):
    shape = mesh.devices.shape
    fine = Mesh(
        mesh.devices.reshape(shape[0], shape[1], shape[2] // MEMBERS, MEMBERS),
        ("clip", "tower", "group", "member"),
    )
    placed = P(("clip", "tower", "group", "member"), None)
    return jax.shard_map(
        body,
        mesh=fine,
        in_specs=(placed,) * 10,
        out_specs=(placed,) * 8,
        check_vma=False,
    )
```

```python
import functools

import jax
import jax.numpy as jnp
from jax import lax
from jax.experimental import pallas as pl
from jax.experimental.pallas import tpu as pltpu
from jax.sharding import Mesh
from jax.sharding import PartitionSpec as P

HEADS = 12
HEAD_SIZE = 128
WINDOW_BLOCKS = 4
HALF_WINDOW = 2
MEMBERS = 4
GROUP_HEADS = HEADS // MEMBERS
GROUP_WIDTH = GROUP_HEADS * HEAD_SIZE
EXTENDED = MEMBERS + WINDOW_BLOCKS - 1
VIDEO = 128
AUDIO = 64
STACK = VIDEO + AUDIO
ROWS = 2 * STACK
LIST_ROWS = 16
SCALE = HEAD_SIZE ** -0.5
LOG2_SCALE = SCALE * 1.4426950408889634
MASKED = -1e30
LARGE = pltpu.CompilerParams(vmem_limit_bytes=60 * 1024 * 1024)
SMALL = pltpu.CompilerParams(vmem_limit_bytes=16 * 1024 * 1024)


def product(left, right, left_dim, right_dim):
    return lax.dot_general(
        left,
        right,
        (((left_dim,), (right_dim,)), ((), ())),
        preferred_element_type=jnp.float32,
    )


PLACES = (
    (1, 0, 128),
    (0, 0, 128),
    (0, 128, 128),
    (1, 128, 64),
    (0, 256, 64),
    (0, 320, 64),
    (1, 192, 128),
    (1, 320, 64),
)


def pack_kernel(shift_ref, video_list, audio_list, *refs):
    arrays, (kv_out, qg_out, sems) = refs[:8], refs[8:]
    copies = []
    for member in range(MEMBERS):
        first = lax.rem(shift_ref[0] + member, MEMBERS) * GROUP_WIDTH
        columns = pl.ds(pl.multiple_of(first, GROUP_WIDTH), GROUP_WIDTH)
        for index, (array, (queried, start, rows)) in enumerate(zip(arrays, PLACES)):
            target = qg_out if queried else kv_out
            copies.append(
                pltpu.make_async_copy(
                    array.at[:, columns],
                    target.at[member, start : start + rows],
                    sems.at[member, index],
                )
            )
            copies[-1].start()
    video_first = jnp.full((8, GROUP_WIDTH), video_list[0, 0].astype(jnp.float32))
    audio_first = jnp.full((8, GROUP_WIDTH), audio_list[0, 0].astype(jnp.float32))
    firsts = jnp.concatenate([video_first, audio_first], axis=0).astype(jnp.bfloat16)
    for member in range(MEMBERS):
        qg_out[member, ROWS : ROWS + LIST_ROWS] = firsts
    for copy in copies:
        copy.wait()


def unpack_kernel(shift_ref, kv, qg, vo, ao, vqg, vkg, vvg, aqg, akg, avg):
    for shift in (0, 1):

        @pl.when(shift_ref[0] == shift)
        def _():
            for member in range(MEMBERS):
                first = (member + shift) % MEMBERS * GROUP_WIDTH
                columns = slice(first, first + GROUP_WIDTH)
                vkg[:, columns] = kv[member, 0:128]
                vvg[:, columns] = kv[member, 128:256]
                akg[:, columns] = kv[member, 256:320]
                avg[:, columns] = kv[member, 320:384]
                vo[:, columns] = qg[member, 0:128]
                ao[:, columns] = qg[member, 128:192]
                vqg[:, columns] = qg[member, 192:320]
                aqg[:, columns] = qg[member, 320:384]


def merge_kernel(own, from_after, from_before, out):
    out[0] = (own[0].astype(jnp.float32) + from_before[...].astype(jnp.float32)).astype(
        jnp.bfloat16
    )
    out[1] = own[1]
    out[2:4] = (own[2:4].astype(jnp.float32) + from_after[...].astype(jnp.float32)).astype(
        jnp.bfloat16
    )


def weights_of(scaled):
    top = jnp.max(scaled, axis=1, keepdims=True)
    powers = jnp.exp2(scaled - top)
    return powers * (1.0 / jnp.sum(powers, axis=1, keepdims=True))


def stacked(parts):
    return parts[0] if len(parts) == 1 else jnp.concatenate(parts, axis=0)


def attention_kernel(
    last_group,
    group_ref,
    kv,
    qg,
    before,
    after,
    qg_out,
    kv_out,
    before_out,
    after_out,
    ak_sum,
    av_sum,
):
    group = group_ref[0]
    sources = [before.at[0], before.at[1]] + [kv.at[m] for m in range(MEMBERS)] + [after]
    targets = [before_out.at[0], before_out.at[1]]
    targets += [kv_out.at[m] for m in range(MEMBERS)] + [after_out]
    ak_sum[...] = jnp.zeros_like(ak_sum)
    av_sum[...] = jnp.zeros_like(av_sum)
    bias_before = jnp.where(group == 0, MASKED, 0.0)
    bias_after = jnp.where(group == last_group, MASKED, 0.0)
    video_slot = lax.broadcasted_iota(jnp.int32, (1, WINDOW_BLOCKS * VIDEO), 1) // VIDEO
    audio_slot = lax.broadcasted_iota(jnp.int32, (1, WINDOW_BLOCKS * AUDIO), 1) // AUDIO
    all_queries, all_cotangents, all_rounded, all_score_grads = [], [], [], []

    for member in range(MEMBERS):
        window_start = group * MEMBERS + member - HALF_WINDOW
        firsts = qg[member, ROWS : ROWS + LIST_ROWS].astype(jnp.float32)
        video_first = jnp.concatenate([firsts[0:1]] * 2, axis=1)
        audio_first = jnp.concatenate([firsts[8:9]] * 4, axis=1)
        video_place = (audio_slot + window_start).astype(jnp.float32) - video_first
        audio_place = (video_slot + window_start).astype(jnp.float32) - audio_first
        cross_bias = jnp.where((video_place == 0.0) | (video_place == 1.0), 0.0, MASKED)
        audio_bias = jnp.where((audio_place == 0.0) | (audio_place == 1.0), 0.0, MASKED)
        queries = qg[member, 0:STACK]
        cotangents = qg[member, STACK:ROWS]
        window = sources[member : member + WINDOW_BLOCKS]
        keys = jnp.concatenate([block[0:128] for block in window], axis=0)
        values = jnp.concatenate([block[128:256] for block in window], axis=0)
        audio_keys = jnp.concatenate([block[256:320] for block in window], axis=0)
        audio_values = jnp.concatenate([block[320:384] for block in window], axis=0)

        scaled = product(queries, keys, 1, 1) * LOG2_SCALE
        video_scaled = scaled[0:VIDEO]
        if member < HALF_WINDOW:
            split = (HALF_WINDOW - member) * VIDEO
            video_scaled = jnp.concatenate(
                [video_scaled[:, :split] + bias_before, video_scaled[:, split:]], axis=1
            )
        elif member == MEMBERS - 1:
            split = (WINDOW_BLOCKS - 1) * VIDEO
            video_scaled = jnp.concatenate(
                [video_scaled[:, :split], video_scaled[:, split:] + bias_after], axis=1
            )
        weights = weights_of(
            jnp.concatenate([video_scaled, scaled[VIDEO:STACK] + audio_bias], axis=0)
        )
        rounded = weights.astype(jnp.bfloat16)
        weight_grad = product(cotangents, values, 1, 1)
        row_dot = jnp.sum(rounded.astype(jnp.float32) * weight_grad, axis=1, keepdims=True)
        score_grad = (weights * (weight_grad - row_dot)).astype(jnp.bfloat16)
        result = product(rounded, values, 1, 0)
        query_term = product(score_grad, keys, 1, 0)
        all_queries.append(queries)
        all_cotangents.append(cotangents)
        all_rounded.append(rounded)
        all_score_grads.append(score_grad)

        video_queries = queries[0:VIDEO]
        video_cotangents = cotangents[0:VIDEO]
        cross_scaled = product(video_queries, audio_keys, 1, 1) * LOG2_SCALE
        cross_weights = weights_of(cross_scaled + cross_bias)
        cross_rounded = cross_weights.astype(jnp.bfloat16)
        cross_grad = product(video_cotangents, audio_values, 1, 1)
        cross_dot = jnp.sum(
            cross_rounded.astype(jnp.float32) * cross_grad, axis=1, keepdims=True
        )
        cross_score_grad = (cross_weights * (cross_grad - cross_dot)).astype(jnp.bfloat16)
        cross_result = product(cross_rounded, audio_values, 1, 0)
        cross_query_term = product(cross_score_grad, audio_keys, 1, 0)
        rows = slice(member * AUDIO, (member + WINDOW_BLOCKS) * AUDIO)
        ak_sum[rows] += product(cross_score_grad, video_queries, 0, 0)
        av_sum[rows] += product(cross_rounded, video_cotangents, 0, 0)

        qg_out[member, 0:128] = (result[0:VIDEO] + cross_result).astype(jnp.bfloat16)
        qg_out[member, 128:192] = result[VIDEO:STACK].astype(jnp.bfloat16)
        qg_out[member, 192:320] = (
            (query_term[0:VIDEO] + cross_query_term) * SCALE
        ).astype(jnp.bfloat16)
        qg_out[member, 320:384] = (query_term[VIDEO:STACK] * SCALE).astype(jnp.bfloat16)

    for block in range(EXTENDED):
        target = targets[block]
        members = [m for m in range(MEMBERS) if 0 <= block - m < WINDOW_BLOCKS]
        columns = {m: slice((block - m) * VIDEO, (block - m + 1) * VIDEO) for m in members}
        score_grads = stacked([all_score_grads[m][:, columns[m]] for m in members])
        rounded = stacked([all_rounded[m][:, columns[m]] for m in members])
        queries = stacked([all_queries[m] for m in members])
        cotangents = stacked([all_cotangents[m] for m in members])
        target[0:128] = (product(score_grads, queries, 0, 0) * SCALE).astype(target.dtype)
        target[128:256] = product(rounded, cotangents, 0, 0).astype(target.dtype)
        rows = slice(block * AUDIO, (block + 1) * AUDIO)
        target[256:320] = (ak_sum[rows] * SCALE).astype(target.dtype)
        target[320:384] = av_sum[rows].astype(target.dtype)


def whole(memory=pltpu.VMEM):
    return pl.BlockSpec(memory_space=memory)


def pack(shift, video_lists, audio_lists, *arrays):
    return pl.pallas_call(
        pack_kernel,
        out_shape=(
            jax.ShapeDtypeStruct((MEMBERS, ROWS, GROUP_WIDTH), jnp.bfloat16),
            jax.ShapeDtypeStruct((MEMBERS, ROWS + LIST_ROWS, GROUP_WIDTH), jnp.bfloat16),
        ),
        in_specs=[whole(pltpu.SMEM)] * 3 + [whole(pl.ANY)] * 8,
        out_specs=(whole(), whole()),
        scratch_shapes=[pltpu.SemaphoreType.DMA((MEMBERS, 8))],
        compiler_params=LARGE,
        name="pack",
    )(shift, video_lists, audio_lists, *arrays)


def unpack(shift, kv, qg):
    video = jax.ShapeDtypeStruct((VIDEO, HEADS * HEAD_SIZE), jnp.bfloat16)
    audio = jax.ShapeDtypeStruct((AUDIO, HEADS * HEAD_SIZE), jnp.bfloat16)
    shapes = (video, audio, video, video, video, audio, audio, audio)
    return pl.pallas_call(
        unpack_kernel,
        out_shape=shapes,
        in_specs=[whole(pltpu.SMEM)] + [whole()] * 2,
        out_specs=[whole()] * 8,
        compiler_params=SMALL,
        name="unpack",
    )(shift, kv, qg)


def merge(own, from_after, from_before):
    return pl.pallas_call(
        merge_kernel,
        out_shape=jax.ShapeDtypeStruct(own.shape, jnp.bfloat16),
        in_specs=[whole()] * 3,
        out_specs=whole(),
        compiler_params=SMALL,
        name="merge",
    )(own, from_after, from_before)


def attention(groups, group, *arrays):
    def head_block(*leading):
        zeros = (0,) * len(leading)
        return pl.BlockSpec(leading + (HEAD_SIZE,), lambda head: zeros + (head,))

    audio_sum = pltpu.VMEM((EXTENDED * AUDIO, HEAD_SIZE), jnp.float32)
    halo = (head_block(HALF_WINDOW, ROWS), head_block(ROWS))
    return pl.pallas_call(
        functools.partial(attention_kernel, groups - 1),
        grid=(GROUP_HEADS,),
        out_shape=(
            jax.ShapeDtypeStruct((MEMBERS, ROWS, GROUP_WIDTH), jnp.bfloat16),
            jax.ShapeDtypeStruct((MEMBERS, ROWS, GROUP_WIDTH), jnp.bfloat16),
            jax.ShapeDtypeStruct((HALF_WINDOW, ROWS, GROUP_WIDTH), jnp.bfloat16),
            jax.ShapeDtypeStruct((ROWS, GROUP_WIDTH), jnp.bfloat16),
        ),
        in_specs=[
            whole(pltpu.SMEM),
            head_block(MEMBERS, ROWS),
            head_block(MEMBERS, ROWS + LIST_ROWS),
            *halo,
        ],
        out_specs=(head_block(MEMBERS, ROWS), head_block(MEMBERS, ROWS), *halo),
        scratch_shapes=[audio_sum, audio_sum],
        compiler_params=LARGE,
        name="attention",
    )(group, *arrays)


def slice_shift(clip, tower, clips):
    return jnp.where((clip == clips - 1) & (tower == 1), 1, 0).astype(jnp.int32).reshape(1)


def to_group(block, distance):
    clips, towers = lax.axis_size("clip"), lax.axis_size("tower")
    per_tower = lax.axis_size("group")
    groups = towers * per_tower
    route = []
    for clip in range(clips):
        for group in range(groups):
            target = group + distance
            if not 0 <= target < groups:
                continue
            turn = target // per_tower - group // per_tower if clip == clips - 1 else 0
            for member in range(MEMBERS):
                route.append(
                    (
                        (clip * groups + group) * MEMBERS + member,
                        (clip * groups + target) * MEMBERS + (member - turn) % MEMBERS,
                    )
                )
    return lax.ppermute(block, ("clip", "tower", "group", "member"), route)


def exchange(packed):
    return lax.all_to_all(packed, "member", 0, 0)


def body(
    video_query,
    video_keys,
    video_value,
    audio_query,
    audio_key,
    audio_value,
    video_cotangent,
    audio_cotangent,
    video_lists,
    audio_lists,
):
    groups = lax.axis_size(("tower", "group"))
    group = lax.axis_index(("tower", "group")).astype(jnp.int32).reshape(1)
    shift = slice_shift(lax.axis_index("clip"), lax.axis_index("tower"), lax.axis_size("clip"))
    kv_packed, qg_packed = pack(
        shift,
        video_lists,
        audio_lists,
        video_query,
        video_keys,
        video_value,
        audio_query,
        audio_key,
        audio_value,
        video_cotangent,
        audio_cotangent,
    )
    kv = exchange(kv_packed)
    before = to_group(kv[MEMBERS - HALF_WINDOW :], 1)
    after = to_group(kv[0], -1)
    qg = exchange(qg_packed)
    qg_part, kv_part, before_part, after_part = attention(
        groups, group, kv, qg, before, after
    )
    qg_back = exchange(qg_part)
    from_after = to_group(before_part, -1)
    from_before = to_group(after_part, 1)
    kv_back = exchange(merge(kv_part, from_after, from_before))
    return unpack(shift, kv_back, qg_back)


def solution(mesh):
    shape = mesh.devices.shape
    fine = Mesh(
        mesh.devices.reshape(shape[0], shape[1], shape[2] // MEMBERS, MEMBERS),
        ("clip", "tower", "group", "member"),
    )
    placed = P(("clip", "tower", "group", "member"), None)
    return jax.shard_map(
        body,
        mesh=fine,
        in_specs=(placed,) * 10,
        out_specs=(placed,) * 8,
        check_vma=False,
    )
```

```python
import functools

import jax
import jax.numpy as jnp
from jax import lax
from jax.experimental import pallas as pl
from jax.experimental.pallas import tpu as pltpu
from jax.sharding import Mesh
from jax.sharding import PartitionSpec as P

HEADS = 12
HEAD_SIZE = 128
WINDOW_BLOCKS = 4
HALF_WINDOW = 2
MEMBERS = 4
GROUP_HEADS = HEADS // MEMBERS
GROUP_WIDTH = GROUP_HEADS * HEAD_SIZE
EXTENDED = MEMBERS + WINDOW_BLOCKS - 1
VIDEO = 128
AUDIO = 64
STACK = VIDEO + AUDIO
ROWS = 2 * STACK
LIST_ROWS = 16
SCALE = HEAD_SIZE ** -0.5
LOG2_SCALE = SCALE * 1.4426950408889634
MASKED = -1e30
LARGE = pltpu.CompilerParams(vmem_limit_bytes=60 * 1024 * 1024)
SMALL = pltpu.CompilerParams(vmem_limit_bytes=16 * 1024 * 1024)


def product(left, right, left_dim, right_dim):
    return lax.dot_general(
        left,
        right,
        (((left_dim,), (right_dim,)), ((), ())),
        preferred_element_type=jnp.float32,
    )


def start_packing(copies, sems, first, arrays, target):
    columns = pl.ds(pl.multiple_of(first, GROUP_WIDTH), GROUP_WIDTH)
    row = 0
    for index, array in enumerate(arrays):
        rows = array.shape[0]
        copy = pltpu.make_async_copy(
            array.at[:, columns], target.at[row : row + rows], sems.at[index]
        )
        copy.start()
        copies.append(copy)
        row += rows


def pack_kv_kernel(place, vk, vv, ak, av, out, sems):
    copies = []
    for member in range(MEMBERS):
        first = lax.rem(place[2] + member, MEMBERS) * GROUP_WIDTH
        start_packing(copies, sems.at[member], first, (vk, vv, ak, av), out.at[member])
    for copy in copies:
        copy.wait()


def pack_qg_kernel(place, video_list, audio_list, vq, aq, vg, ag, out, sems):
    copies = []
    for member in range(MEMBERS):
        first = lax.rem(place[2] + member, MEMBERS) * GROUP_WIDTH
        start_packing(copies, sems.at[member], first, (vq, aq, vg, ag), out.at[member])
    video_first = jnp.full((8, GROUP_WIDTH), video_list[0, 0].astype(jnp.float32))
    audio_first = jnp.full((8, GROUP_WIDTH), audio_list[0, 0].astype(jnp.float32))
    firsts = jnp.concatenate([video_first, audio_first], axis=0).astype(jnp.bfloat16)
    for member in range(MEMBERS):
        out[member, ROWS : ROWS + LIST_ROWS] = firsts
    for copy in copies:
        copy.wait()


def unpack_kernel(place, kv, qg, vo, ao, vqg, vkg, vvg, aqg, akg, avg):
    for member in range(MEMBERS):
        first = lax.rem(place[2] + member, MEMBERS) * GROUP_WIDTH
        columns = pl.ds(pl.multiple_of(first, GROUP_WIDTH), GROUP_WIDTH)
        vo[:, columns] = qg[member, 0:128]
        ao[:, columns] = qg[member, 128:192]
        vqg[:, columns] = qg[member, 192:320]
        aqg[:, columns] = qg[member, 320:384]
        vkg[:, columns] = kv[member, 0:128]
        vvg[:, columns] = kv[member, 128:256]
        akg[:, columns] = kv[member, 256:320]
        avg[:, columns] = kv[member, 320:384]


def merge_kernel(own, from_after, from_before, out):
    out[0] = (own[0].astype(jnp.float32) + from_before[...].astype(jnp.float32)).astype(
        jnp.bfloat16
    )
    out[1] = own[1]
    out[2:4] = (own[2:4].astype(jnp.float32) + from_after[...].astype(jnp.float32)).astype(
        jnp.bfloat16
    )


def stacked(parts):
    return parts[0] if len(parts) == 1 else jnp.concatenate(parts, axis=0)


def masks_of(window_start, firsts):
    firsts = firsts.astype(jnp.float32)
    video_slot = lax.broadcasted_iota(jnp.int32, (1, WINDOW_BLOCKS * VIDEO), 1) // VIDEO
    audio_slot = lax.broadcasted_iota(jnp.int32, (1, WINDOW_BLOCKS * AUDIO), 1) // AUDIO
    video_first = jnp.concatenate([firsts[0:1]] * 2, axis=1)
    audio_first = jnp.concatenate([firsts[8:9]] * 4, axis=1)
    video_place = (audio_slot + window_start).astype(jnp.float32) - video_first
    audio_place = (video_slot + window_start).astype(jnp.float32) - audio_first
    cross_mask = jnp.where((video_place == 0.0) | (video_place == 1.0), 0.0, MASKED)
    audio_mask = jnp.where((audio_place == 0.0) | (audio_place == 1.0), 0.0, MASKED)
    return cross_mask, audio_mask


def softmax_and_grad(scaled, weight_grad):
    top = [jnp.max(s, axis=1, keepdims=True) for s in scaled]
    powers = [jnp.exp2(s - t) for s, t in zip(scaled, top)]
    scale = [1.0 / jnp.sum(p, axis=1, keepdims=True) for p in powers]
    weights = [p * s for p, s in zip(powers, scale)]
    rounded = [w.astype(jnp.bfloat16) for w in weights]
    row_dot = [
        jnp.sum(r.astype(jnp.float32) * g, axis=1, keepdims=True)
        for r, g in zip(rounded, weight_grad)
    ]
    score_grad = [
        (w * (g - d)).astype(jnp.bfloat16) for w, g, d in zip(weights, weight_grad, row_dot)
    ]
    return rounded, score_grad


def attention_kernel(
    last_group, place, kv, qg, before, after, qg_out, kv_out, before_out, after_out
):
    group = place[0]
    members = range(MEMBERS)
    sources = [before.at[0], before.at[1]] + [kv.at[m] for m in members] + [after]
    targets = [before_out.at[0], before_out.at[1]]
    targets += [kv_out.at[m] for m in members] + [after_out]
    bias_before = jnp.where(group == 0, MASKED, 0.0)
    bias_after = jnp.where(group == last_group, MASKED, 0.0)

    queries = [qg[m, 0:STACK] for m in members]
    cotangents = [qg[m, STACK:ROWS] for m in members]
    video_queries = [q[0:VIDEO] for q in queries]
    video_cotangents = [g[0:VIDEO] for g in cotangents]
    windows = [sources[m : m + WINDOW_BLOCKS] for m in members]
    keys = [jnp.concatenate([b[0:128] for b in w], axis=0) for w in windows]
    values = [jnp.concatenate([b[128:256] for b in w], axis=0) for w in windows]
    audio_keys = [jnp.concatenate([b[256:320] for b in w], axis=0) for w in windows]
    audio_values = [jnp.concatenate([b[320:384] for b in w], axis=0) for w in windows]

    rounded, score_grads, cross_rounded, cross_score_grads = [], [], [], []
    for m in members:
        cross_mask, audio_mask = masks_of(
            group * MEMBERS + m - HALF_WINDOW, qg[m, ROWS : ROWS + LIST_ROWS]
        )
        scaled = product(queries[m], keys[m], 1, 1) * LOG2_SCALE
        cross_scaled = product(video_queries[m], audio_keys[m], 1, 1) * LOG2_SCALE
        video_scaled = scaled[0:VIDEO]
        if m < HALF_WINDOW:
            split = (HALF_WINDOW - m) * VIDEO
            video_scaled = jnp.concatenate(
                [video_scaled[:, :split] + bias_before, video_scaled[:, split:]], axis=1
            )
        elif m == MEMBERS - 1:
            split = (WINDOW_BLOCKS - 1) * VIDEO
            video_scaled = jnp.concatenate(
                [video_scaled[:, :split], video_scaled[:, split:] + bias_after], axis=1
            )
        scaled = jnp.concatenate([video_scaled, scaled[VIDEO:STACK] + audio_mask], axis=0)
        weight_grad = product(cotangents[m], values[m], 1, 1)
        cross_grad = product(video_cotangents[m], audio_values[m], 1, 1)
        (r, cr), (s, cs) = softmax_and_grad(
            (scaled, cross_scaled + cross_mask), (weight_grad, cross_grad)
        )
        rounded.append(r)
        score_grads.append(s)
        cross_rounded.append(cr)
        cross_score_grads.append(cs)

    result = [product(rounded[m], values[m], 1, 0) for m in members]
    cross_result = [product(cross_rounded[m], audio_values[m], 1, 0) for m in members]
    query_term = [product(score_grads[m], keys[m], 1, 0) for m in members]
    cross_query = [product(cross_score_grads[m], audio_keys[m], 1, 0) for m in members]
    ak_terms = [product(cross_score_grads[m], video_queries[m], 0, 0) for m in members]
    av_terms = [product(cross_rounded[m], video_cotangents[m], 0, 0) for m in members]
    for m in members:
        qg_out[m, 0:128] = (result[m][0:VIDEO] + cross_result[m]).astype(jnp.bfloat16)
        qg_out[m, 128:192] = result[m][VIDEO:STACK].astype(jnp.bfloat16)
        qg_out[m, 192:320] = (
            (query_term[m][0:VIDEO] + cross_query[m]) * SCALE
        ).astype(jnp.bfloat16)
        qg_out[m, 320:384] = (query_term[m][VIDEO:STACK] * SCALE).astype(jnp.bfloat16)

    for block in range(EXTENDED):
        target = targets[block]
        users = [m for m in members if 0 <= block - m < WINDOW_BLOCKS]
        columns = {m: slice((block - m) * VIDEO, (block - m + 1) * VIDEO) for m in users}
        rows = {m: slice((block - m) * AUDIO, (block - m + 1) * AUDIO) for m in users}
        vk_sum = product(
            stacked([score_grads[m][:, columns[m]] for m in users]),
            stacked([queries[m] for m in users]),
            0,
            0,
        )
        vv_sum = product(
            stacked([rounded[m][:, columns[m]] for m in users]),
            stacked([cotangents[m] for m in users]),
            0,
            0,
        )
        ak_sum = sum(ak_terms[m][rows[m]] for m in users)
        av_sum = sum(av_terms[m][rows[m]] for m in users)
        target[0:128] = (vk_sum * SCALE).astype(target.dtype)
        target[128:256] = vv_sum.astype(target.dtype)
        target[256:320] = (ak_sum * SCALE).astype(target.dtype)
        target[320:384] = av_sum.astype(target.dtype)


def whole(memory=pltpu.VMEM):
    return pl.BlockSpec(memory_space=memory)


PACKED_KV = jax.ShapeDtypeStruct((MEMBERS, ROWS, GROUP_WIDTH), jnp.bfloat16)
BLOCK_KV = jax.ShapeDtypeStruct((ROWS, GROUP_WIDTH), jnp.bfloat16)
PACKED_QG = jax.ShapeDtypeStruct((MEMBERS, ROWS + LIST_ROWS, GROUP_WIDTH), jnp.bfloat16)


def pack_kv(place, *arrays):
    return pl.pallas_call(
        pack_kv_kernel,
        out_shape=PACKED_KV,
        in_specs=[whole(pltpu.SMEM)] + [whole(pl.ANY)] * 4,
        out_specs=whole(),
        scratch_shapes=[pltpu.SemaphoreType.DMA((MEMBERS, 4))],
        compiler_params=LARGE,
        name="pack_kv",
    )(place, *arrays)


def pack_qg(place, *arrays):
    return pl.pallas_call(
        pack_qg_kernel,
        out_shape=PACKED_QG,
        in_specs=[whole(pltpu.SMEM)] * 3 + [whole(pl.ANY)] * 4,
        out_specs=whole(),
        scratch_shapes=[pltpu.SemaphoreType.DMA((MEMBERS, 4))],
        compiler_params=LARGE,
        name="pack_qg",
    )(place, *arrays)


def unpack(place, kv, qg):
    video = jax.ShapeDtypeStruct((VIDEO, HEADS * HEAD_SIZE), jnp.bfloat16)
    audio = jax.ShapeDtypeStruct((AUDIO, HEADS * HEAD_SIZE), jnp.bfloat16)
    shapes = (video, audio, video, video, video, audio, audio, audio)
    return pl.pallas_call(
        unpack_kernel,
        out_shape=shapes,
        in_specs=[whole(pltpu.SMEM)] + [whole()] * 2,
        out_specs=[whole()] * 8,
        compiler_params=SMALL,
        name="unpack",
    )(place, kv, qg)


def merge(own, from_after, from_before):
    return pl.pallas_call(
        merge_kernel,
        out_shape=PACKED_KV,
        in_specs=[whole()] * 3,
        out_specs=whole(),
        compiler_params=SMALL,
        name="merge",
    )(own, from_after, from_before)


def attention(groups, place, kv, qg, before, after):
    def head_block(*leading):
        zeros = (0,) * len(leading)
        return pl.BlockSpec(leading + (HEAD_SIZE,), lambda head: zeros + (head,))

    halo = (head_block(HALF_WINDOW, ROWS), head_block(ROWS))
    return pl.pallas_call(
        functools.partial(attention_kernel, groups - 1),
        grid=(GROUP_HEADS,),
        out_shape=(
            PACKED_KV,
            PACKED_KV,
            jax.ShapeDtypeStruct((HALF_WINDOW, ROWS, GROUP_WIDTH), jnp.bfloat16),
            BLOCK_KV,
        ),
        in_specs=[
            whole(pltpu.SMEM),
            head_block(MEMBERS, ROWS),
            head_block(MEMBERS, ROWS + LIST_ROWS),
            *halo,
        ],
        out_specs=(head_block(MEMBERS, ROWS), head_block(MEMBERS, ROWS), *halo),
        compiler_params=LARGE,
        name="attention",
    )(place, kv, qg, before, after)


def place_of():
    clip, tower = lax.axis_index("clip"), lax.axis_index("tower")
    group, member = lax.axis_index(("tower", "group")), lax.axis_index("member")
    shifted = (clip == lax.axis_size("clip") - 1) & (tower == 1)
    return jnp.stack([group, member, shifted.astype(jnp.int32)]).astype(jnp.int32)


def to_group(block, distance):
    clips, towers = lax.axis_size("clip"), lax.axis_size("tower")
    per_tower = lax.axis_size("group")
    groups = towers * per_tower
    route = []
    for clip in range(clips):
        for group in range(groups):
            target = group + distance
            if not 0 <= target < groups:
                continue
            turn = target // per_tower - group // per_tower if clip == clips - 1 else 0
            for member in range(MEMBERS):
                route.append(
                    (
                        (clip * groups + group) * MEMBERS + member,
                        (clip * groups + target) * MEMBERS + (member - turn) % MEMBERS,
                    )
                )
    return lax.ppermute(block, ("clip", "tower", "group", "member"), route)


def exchange(packed):
    return lax.all_to_all(packed, "member", 0, 0)


def body(
    video_query,
    video_keys,
    video_value,
    audio_query,
    audio_key,
    audio_value,
    video_cotangent,
    audio_cotangent,
    video_lists,
    audio_lists,
):
    groups = lax.axis_size(("tower", "group"))
    place = place_of()
    kv_packed = pack_kv(place, video_keys, video_value, audio_key, audio_value)
    kv = exchange(kv_packed)
    qg_packed = pack_qg(
        place,
        video_lists,
        audio_lists,
        video_query,
        audio_query,
        video_cotangent,
        audio_cotangent,
    )
    before = to_group(kv[MEMBERS - HALF_WINDOW :], 1)
    after = to_group(kv[0], -1)
    qg = exchange(qg_packed)
    qg_part, kv_part, before_part, after_part = attention(
        groups, place, kv, qg, before, after
    )
    qg_back = exchange(qg_part)
    from_after = to_group(before_part, -1)
    from_before = to_group(after_part, 1)
    kv_back = exchange(merge(kv_part, from_after, from_before))
    return unpack(place, kv_back, qg_back)


def solution(mesh):
    shape = mesh.devices.shape
    fine = Mesh(
        mesh.devices.reshape(shape[0], shape[1], shape[2] // MEMBERS, MEMBERS),
        ("clip", "tower", "group", "member"),
    )
    placed = P(("clip", "tower", "group", "member"), None)
    return jax.shard_map(
        body,
        mesh=fine,
        in_specs=(placed,) * 10,
        out_specs=(placed,) * 8,
        check_vma=False,
    )
```

```python
import functools

import jax
import jax.numpy as jnp
from jax import lax
from jax.experimental import pallas as pl
from jax.experimental.pallas import tpu as pltpu
from jax.sharding import Mesh
from jax.sharding import PartitionSpec as P

HEADS = 12
HEAD_SIZE = 128
WINDOW_BLOCKS = 4
HALF_WINDOW = 2
MEMBERS = 4
GROUP_HEADS = HEADS // MEMBERS
GROUP_WIDTH = GROUP_HEADS * HEAD_SIZE
EXTENDED = MEMBERS + WINDOW_BLOCKS - 1
VIDEO = 128
AUDIO = 64
STACK = VIDEO + AUDIO
ROWS = 2 * STACK
LIST_ROWS = 16
SCALE = HEAD_SIZE ** -0.5
LOG2_SCALE = SCALE * 1.4426950408889634
MASKED = -1e30
LARGE = pltpu.CompilerParams(vmem_limit_bytes=60 * 1024 * 1024)
SMALL = pltpu.CompilerParams(vmem_limit_bytes=16 * 1024 * 1024)


def product(left, right, left_dim, right_dim):
    return lax.dot_general(
        left,
        right,
        (((left_dim,), (right_dim,)), ((), ())),
        preferred_element_type=jnp.float32,
    )


def start_packing(copies, sems, first, arrays, target):
    columns = pl.ds(pl.multiple_of(first, GROUP_WIDTH), GROUP_WIDTH)
    row = 0
    for index, array in enumerate(arrays):
        rows = array.shape[0]
        copy = pltpu.make_async_copy(
            array.at[:, columns], target.at[row : row + rows], sems.at[index]
        )
        copy.start()
        copies.append(copy)
        row += rows


def pack_kv_kernel(shift, vk, vv, ak, av, out, sems):
    copies = []
    for member in range(MEMBERS):
        first = lax.rem(shift[0] + member, MEMBERS) * GROUP_WIDTH
        start_packing(copies, sems.at[member], first, (vk, vv, ak, av), out.at[member])
    for copy in copies:
        copy.wait()


def pack_qg_kernel(shift, video_list, audio_list, vq, aq, vg, ag, out, sems):
    copies = []
    for member in range(MEMBERS):
        first = lax.rem(shift[0] + member, MEMBERS) * GROUP_WIDTH
        start_packing(copies, sems.at[member], first, (vq, aq, vg, ag), out.at[member])
    video_first = jnp.full((8, GROUP_WIDTH), video_list[0, 0].astype(jnp.float32))
    audio_first = jnp.full((8, GROUP_WIDTH), audio_list[0, 0].astype(jnp.float32))
    firsts = jnp.concatenate([video_first, audio_first], axis=0).astype(jnp.bfloat16)
    for member in range(MEMBERS):
        out[member, ROWS : ROWS + LIST_ROWS] = firsts
    for copy in copies:
        copy.wait()


def unpack_kernel(shift, kv, qg, vo, ao, vqg, vkg, vvg, aqg, akg, avg):
    for member in range(MEMBERS):
        first = lax.rem(shift[0] + member, MEMBERS) * GROUP_WIDTH
        columns = pl.ds(pl.multiple_of(first, GROUP_WIDTH), GROUP_WIDTH)
        vo[:, columns] = qg[member, 0:128]
        ao[:, columns] = qg[member, 128:192]
        vqg[:, columns] = qg[member, 192:320]
        aqg[:, columns] = qg[member, 320:384]
        vkg[:, columns] = kv[member, 0:128]
        vvg[:, columns] = kv[member, 128:256]
        akg[:, columns] = kv[member, 256:320]
        avg[:, columns] = kv[member, 320:384]


def merge_kernel(
    last_group, group_ref, own, from_after_2, from_after_3, relayed_3, from_before, out
):
    def total(member, *received):
        parts = [own[member].astype(jnp.float32)]
        parts += [r[...].astype(jnp.float32) for r in received]
        out[member] = sum(parts).astype(jnp.bfloat16)

    total(0, from_before)
    out[1] = own[1]
    total(2, from_after_2)
    total(3, relayed_3)

    @pl.when(group_ref[0] != last_group)
    def _():
        total(3, from_after_3, relayed_3)


def stacked(parts):
    return parts[0] if len(parts) == 1 else jnp.concatenate(parts, axis=0)


def masks_of(window_start, firsts):
    firsts = firsts.astype(jnp.float32)
    video_slot = lax.broadcasted_iota(jnp.int32, (1, WINDOW_BLOCKS * VIDEO), 1) // VIDEO
    audio_slot = lax.broadcasted_iota(jnp.int32, (1, WINDOW_BLOCKS * AUDIO), 1) // AUDIO
    video_first = jnp.concatenate([firsts[0:1]] * 2, axis=1)
    audio_first = jnp.concatenate([firsts[8:9]] * 4, axis=1)
    video_place = (audio_slot + window_start).astype(jnp.float32) - video_first
    audio_place = (video_slot + window_start).astype(jnp.float32) - audio_first
    cross_mask = jnp.where((video_place == 0.0) | (video_place == 1.0), 0.0, MASKED)
    audio_mask = jnp.where((audio_place == 0.0) | (audio_place == 1.0), 0.0, MASKED)
    return cross_mask, audio_mask


def softmax_and_grad(scaled, weight_grad):
    top = [jnp.max(s, axis=1, keepdims=True) for s in scaled]
    powers = [jnp.exp2(s - t) for s, t in zip(scaled, top)]
    scale = [1.0 / jnp.sum(p, axis=1, keepdims=True) for p in powers]
    weights = [p * s for p, s in zip(powers, scale)]
    rounded = [w.astype(jnp.bfloat16) for w in weights]
    row_dot = [
        jnp.sum(r.astype(jnp.float32) * g, axis=1, keepdims=True)
        for r, g in zip(rounded, weight_grad)
    ]
    score_grad = [
        (w * (g - d)).astype(jnp.bfloat16) for w, g, d in zip(weights, weight_grad, row_dot)
    ]
    return rounded, score_grad


def attention_kernel(
    last_group,
    group_ref,
    kv,
    qg,
    before_2,
    before_3,
    relayed_3,
    after,
    qg_out,
    kv_out,
    before_2_out,
    before_3_out,
    after_out,
    before_sum,
):
    group = group_ref[0]
    before_sum[...] = before_3[...] + relayed_3[...]
    members = range(MEMBERS)
    sources = [before_2, before_sum] + [kv.at[m] for m in members] + [after]
    targets = [before_2_out, before_3_out] + [kv_out.at[m] for m in members] + [after_out]
    bias_before = jnp.where(group == 0, MASKED, 0.0)
    bias_after = jnp.where(group == last_group, MASKED, 0.0)

    queries = [qg[m, 0:STACK] for m in members]
    cotangents = [qg[m, STACK:ROWS] for m in members]
    video_queries = [q[0:VIDEO] for q in queries]
    video_cotangents = [g[0:VIDEO] for g in cotangents]
    windows = [sources[m : m + WINDOW_BLOCKS] for m in members]
    keys = [jnp.concatenate([b[0:128] for b in w], axis=0) for w in windows]
    values = [jnp.concatenate([b[128:256] for b in w], axis=0) for w in windows]
    audio_keys = [jnp.concatenate([b[256:320] for b in w], axis=0) for w in windows]
    audio_values = [jnp.concatenate([b[320:384] for b in w], axis=0) for w in windows]

    rounded, score_grads, cross_rounded, cross_score_grads = [], [], [], []
    for m in members:
        cross_mask, audio_mask = masks_of(
            group * MEMBERS + m - HALF_WINDOW, qg[m, ROWS : ROWS + LIST_ROWS]
        )
        scaled = product(queries[m], keys[m], 1, 1) * LOG2_SCALE
        cross_scaled = product(video_queries[m], audio_keys[m], 1, 1) * LOG2_SCALE
        video_scaled = scaled[0:VIDEO]
        if m < HALF_WINDOW:
            split = (HALF_WINDOW - m) * VIDEO
            video_scaled = jnp.concatenate(
                [video_scaled[:, :split] + bias_before, video_scaled[:, split:]], axis=1
            )
        elif m == MEMBERS - 1:
            split = (WINDOW_BLOCKS - 1) * VIDEO
            video_scaled = jnp.concatenate(
                [video_scaled[:, :split], video_scaled[:, split:] + bias_after], axis=1
            )
        scaled = jnp.concatenate([video_scaled, scaled[VIDEO:STACK] + audio_mask], axis=0)
        weight_grad = product(cotangents[m], values[m], 1, 1)
        cross_grad = product(video_cotangents[m], audio_values[m], 1, 1)
        (r, cr), (s, cs) = softmax_and_grad(
            (scaled, cross_scaled + cross_mask), (weight_grad, cross_grad)
        )
        rounded.append(r)
        score_grads.append(s)
        cross_rounded.append(cr)
        cross_score_grads.append(cs)

    result = [product(rounded[m], values[m], 1, 0) for m in members]
    cross_result = [product(cross_rounded[m], audio_values[m], 1, 0) for m in members]
    query_term = [product(score_grads[m], keys[m], 1, 0) for m in members]
    cross_query = [product(cross_score_grads[m], audio_keys[m], 1, 0) for m in members]
    ak_terms = [product(cross_score_grads[m], video_queries[m], 0, 0) for m in members]
    av_terms = [product(cross_rounded[m], video_cotangents[m], 0, 0) for m in members]
    for m in members:
        qg_out[m, 0:128] = (result[m][0:VIDEO] + cross_result[m]).astype(jnp.bfloat16)
        qg_out[m, 128:192] = result[m][VIDEO:STACK].astype(jnp.bfloat16)
        qg_out[m, 192:320] = (
            (query_term[m][0:VIDEO] + cross_query[m]) * SCALE
        ).astype(jnp.bfloat16)
        qg_out[m, 320:384] = (query_term[m][VIDEO:STACK] * SCALE).astype(jnp.bfloat16)

    for block in range(EXTENDED):
        target = targets[block]
        users = [m for m in members if 0 <= block - m < WINDOW_BLOCKS]
        columns = {m: slice((block - m) * VIDEO, (block - m + 1) * VIDEO) for m in users}
        rows = {m: slice((block - m) * AUDIO, (block - m + 1) * AUDIO) for m in users}
        vk_sum = product(
            stacked([score_grads[m][:, columns[m]] for m in users]),
            stacked([queries[m] for m in users]),
            0,
            0,
        )
        vv_sum = product(
            stacked([rounded[m][:, columns[m]] for m in users]),
            stacked([cotangents[m] for m in users]),
            0,
            0,
        )
        ak_sum = sum(ak_terms[m][rows[m]] for m in users)
        av_sum = sum(av_terms[m][rows[m]] for m in users)
        target[0:128] = (vk_sum * SCALE).astype(target.dtype)
        target[128:256] = vv_sum.astype(target.dtype)
        target[256:320] = (ak_sum * SCALE).astype(target.dtype)
        target[320:384] = av_sum.astype(target.dtype)


def whole(memory=pltpu.VMEM):
    return pl.BlockSpec(memory_space=memory)


PACKED_KV = jax.ShapeDtypeStruct((MEMBERS, ROWS, GROUP_WIDTH), jnp.bfloat16)
BLOCK_KV = jax.ShapeDtypeStruct((ROWS, GROUP_WIDTH), jnp.bfloat16)
PACKED_QG = jax.ShapeDtypeStruct((MEMBERS, ROWS + LIST_ROWS, GROUP_WIDTH), jnp.bfloat16)


def pack_kv(shift, *arrays):
    return pl.pallas_call(
        pack_kv_kernel,
        out_shape=PACKED_KV,
        in_specs=[whole(pltpu.SMEM)] + [whole(pl.ANY)] * 4,
        out_specs=whole(),
        scratch_shapes=[pltpu.SemaphoreType.DMA((MEMBERS, 4))],
        compiler_params=LARGE,
        name="pack_kv",
    )(shift, *arrays)


def pack_qg(shift, *arrays):
    return pl.pallas_call(
        pack_qg_kernel,
        out_shape=PACKED_QG,
        in_specs=[whole(pltpu.SMEM)] * 3 + [whole(pl.ANY)] * 4,
        out_specs=whole(),
        scratch_shapes=[pltpu.SemaphoreType.DMA((MEMBERS, 4))],
        compiler_params=LARGE,
        name="pack_qg",
    )(shift, *arrays)


def unpack(shift, kv, qg):
    video = jax.ShapeDtypeStruct((VIDEO, HEADS * HEAD_SIZE), jnp.bfloat16)
    audio = jax.ShapeDtypeStruct((AUDIO, HEADS * HEAD_SIZE), jnp.bfloat16)
    shapes = (video, audio, video, video, video, audio, audio, audio)
    return pl.pallas_call(
        unpack_kernel,
        out_shape=shapes,
        in_specs=[whole(pltpu.SMEM)] + [whole()] * 2,
        out_specs=[whole()] * 8,
        compiler_params=SMALL,
        name="unpack",
    )(shift, kv, qg)


def merge(groups, group, *arrays):
    return pl.pallas_call(
        functools.partial(merge_kernel, groups - 1),
        out_shape=PACKED_KV,
        in_specs=[whole(pltpu.SMEM)] + [whole()] * 5,
        out_specs=whole(),
        compiler_params=SMALL,
        name="merge",
    )(group, *arrays)


def attention(groups, group, *arrays):
    def head_block(*leading):
        zeros = (0,) * len(leading)
        return pl.BlockSpec(leading + (HEAD_SIZE,), lambda head: zeros + (head,))

    return pl.pallas_call(
        functools.partial(attention_kernel, groups - 1),
        grid=(GROUP_HEADS,),
        out_shape=[PACKED_KV] * 2 + [BLOCK_KV] * 3,
        in_specs=[
            whole(pltpu.SMEM),
            head_block(MEMBERS, ROWS),
            head_block(MEMBERS, ROWS + LIST_ROWS),
            *[head_block(ROWS)] * 4,
        ],
        out_specs=[head_block(MEMBERS, ROWS)] * 2 + [head_block(ROWS)] * 3,
        scratch_shapes=[pltpu.VMEM((ROWS, HEAD_SIZE), jnp.bfloat16)],
        compiler_params=LARGE,
        name="attention",
    )(group, *arrays)


def slice_shift():
    clip, tower = lax.axis_index("clip"), lax.axis_index("tower")
    shifted = (clip == lax.axis_size("clip") - 1) & (tower == 1)
    return jnp.where(shifted, 1, 0).astype(jnp.int32).reshape(1)


def moved(block, hops):
    clips, towers = lax.axis_size("clip"), lax.axis_size("tower")
    per_tower = lax.axis_size("group")
    route = []
    for clip in range(clips):
        for group, target in hops:
            turn = target // per_tower - group // per_tower if clip == clips - 1 else 0
            for member in range(MEMBERS):
                route.append(
                    (
                        (clip * towers * per_tower + group) * MEMBERS + member,
                        (clip * towers * per_tower + target) * MEMBERS
                        + (member - turn) % MEMBERS,
                    )
                )
    return lax.ppermute(block, ("clip", "tower", "group", "member"), route)


def to_group(block, distance):
    groups = lax.axis_size(("tower", "group"))
    hops = [(g, g + distance) for g in range(groups) if 0 <= g + distance < groups]
    return moved(block, hops)


def to_group_by_relay(block, distance):
    groups, per_tower = lax.axis_size(("tower", "group")), lax.axis_size("group")
    relay = 0 if distance > 0 else groups - 1
    first, second = [], []
    for group in range(groups):
        target = group + distance
        if not 0 <= target < groups:
            continue
        if group // per_tower == target // per_tower:
            first.append((group, target))
        else:
            first.append((group, relay))
            second.append((relay, target))
    arrived = moved(block, first)
    return arrived, moved(arrived, second)


def exchange(packed):
    return lax.all_to_all(packed, "member", 0, 0)


def body(
    video_query,
    video_keys,
    video_value,
    audio_query,
    audio_key,
    audio_value,
    video_cotangent,
    audio_cotangent,
    video_lists,
    audio_lists,
):
    groups = lax.axis_size(("tower", "group"))
    group = lax.axis_index(("tower", "group")).astype(jnp.int32).reshape(1)
    shift = slice_shift()
    kv_packed = pack_kv(shift, video_keys, video_value, audio_key, audio_value)
    kv = exchange(kv_packed)
    qg_packed = pack_qg(
        shift,
        video_lists,
        audio_lists,
        video_query,
        audio_query,
        video_cotangent,
        audio_cotangent,
    )
    before_3, relayed_3 = to_group_by_relay(kv[3], 1)
    before_2 = to_group(kv[2], 1)
    after = to_group(kv[0], -1)
    qg = exchange(qg_packed)
    qg_part, kv_part, part_2, part_3, after_part = attention(
        groups, group, kv, qg, before_2, before_3, relayed_3, after
    )
    qg_back = exchange(qg_part)
    from_after_3, relayed_back = to_group_by_relay(part_3, -1)
    from_after_2 = to_group(part_2, -1)
    from_before = to_group(after_part, 1)
    merged = merge(
        groups, group, kv_part, from_after_2, from_after_3, relayed_back, from_before
    )
    kv_back = exchange(merged)
    return unpack(shift, kv_back, qg_back)


def solution(mesh):
    shape = mesh.devices.shape
    fine = Mesh(
        mesh.devices.reshape(shape[0], shape[1], shape[2] // MEMBERS, MEMBERS),
        ("clip", "tower", "group", "member"),
    )
    placed = P(("clip", "tower", "group", "member"), None)
    return jax.shard_map(
        body,
        mesh=fine,
        in_specs=(placed,) * 10,
        out_specs=(placed,) * 8,
        check_vma=False,
    )
```

```python
import functools

import jax
import jax.numpy as jnp
from jax import lax
from jax.experimental import pallas as pl
from jax.experimental.pallas import tpu as pltpu
from jax.sharding import Mesh
from jax.sharding import PartitionSpec as P

HEADS = 12
HEAD_SIZE = 128
WINDOW_BLOCKS = 4
HALF_WINDOW = 2
MEMBERS = 4
GROUP_HEADS = HEADS // MEMBERS
GROUP_WIDTH = GROUP_HEADS * HEAD_SIZE
EXTENDED = MEMBERS + WINDOW_BLOCKS - 1
VIDEO = 128
AUDIO = 64
STACK = VIDEO + AUDIO
ROWS = 2 * STACK
LIST_ROWS = 16
SCALE = HEAD_SIZE ** -0.5
LOG2_SCALE = SCALE * 1.4426950408889634
MASKED = -1e30
LARGE = pltpu.CompilerParams(vmem_limit_bytes=60 * 1024 * 1024)
SMALL = pltpu.CompilerParams(vmem_limit_bytes=16 * 1024 * 1024)


def product(left, right, left_dim, right_dim):
    return lax.dot_general(
        left,
        right,
        (((left_dim,), (right_dim,)), ((), ())),
        preferred_element_type=jnp.float32,
    )


def start_packing(copies, sems, first, arrays, target):
    columns = pl.ds(pl.multiple_of(first, GROUP_WIDTH), GROUP_WIDTH)
    row = 0
    for index, array in enumerate(arrays):
        rows = array.shape[0]
        copy = pltpu.make_async_copy(
            array.at[:, columns], target.at[row : row + rows], sems.at[index]
        )
        copy.start()
        copies.append(copy)
        row += rows


def pack_kv_kernel(shift, vk, vv, ak, av, out, sems):
    copies = []
    for member in range(MEMBERS):
        first = lax.rem(shift[0] + member, MEMBERS) * GROUP_WIDTH
        start_packing(copies, sems.at[member], first, (vk, vv, ak, av), out.at[member])
    for copy in copies:
        copy.wait()


def pack_qg_kernel(shift, video_list, audio_list, vq, aq, vg, ag, out, sems):
    copies = []
    for member in range(MEMBERS):
        first = lax.rem(shift[0] + member, MEMBERS) * GROUP_WIDTH
        start_packing(copies, sems.at[member], first, (vq, aq, vg, ag), out.at[member])
    video_first = jnp.full((8, GROUP_WIDTH), video_list[0, 0].astype(jnp.float32))
    audio_first = jnp.full((8, GROUP_WIDTH), audio_list[0, 0].astype(jnp.float32))
    firsts = jnp.concatenate([video_first, audio_first], axis=0).astype(jnp.bfloat16)
    for member in range(MEMBERS):
        out[member, ROWS : ROWS + LIST_ROWS] = firsts
    for copy in copies:
        copy.wait()


def unpack_rows(packed, columns, outs):
    row = 0
    for out in outs:
        rows = out.shape[0]
        out[:, columns] = packed[row : row + rows]
        row += rows


def columns_of(member):
    first = lax.rem(member, MEMBERS) * GROUP_WIDTH
    return pl.ds(pl.multiple_of(first, GROUP_WIDTH), GROUP_WIDTH)


def unpack_qg_kernel(shift, packed, *outs):
    for member in range(MEMBERS):
        unpack_rows(packed.at[member], columns_of(shift[0] + member), outs)


def unpack_kv_kernel(shift, me, *refs):
    blocks, outs = refs[:MEMBERS], refs[MEMBERS:]
    for distance, block in enumerate(blocks):
        unpack_rows(block, columns_of(shift[0] + me[0] + MEMBERS - distance), outs)


def merge_kernel(
    last_group, group_ref, me, own, from_after_2, from_after_3, relayed_3, from_before, *refs
):
    outs, out = refs[:MEMBERS], refs[MEMBERS]

    def total(member, *received):
        parts = [own[member].astype(jnp.float32)]
        parts += [r[...].astype(jnp.float32) for r in received]
        out[member] = sum(parts).astype(jnp.bfloat16)

    total(0, from_before)
    out[1] = own[1]
    total(2, from_after_2)
    total(3, relayed_3)

    @pl.when(group_ref[0] != last_group)
    def _():
        total(3, from_after_3, relayed_3)

    for distance, target in enumerate(outs):
        target[...] = out[lax.rem(me[0] + distance, MEMBERS)]


def stacked(parts):
    return parts[0] if len(parts) == 1 else jnp.concatenate(parts, axis=0)


def masks_of(window_start, firsts):
    firsts = firsts.astype(jnp.float32)
    video_slot = lax.broadcasted_iota(jnp.int32, (1, WINDOW_BLOCKS * VIDEO), 1) // VIDEO
    audio_slot = lax.broadcasted_iota(jnp.int32, (1, WINDOW_BLOCKS * AUDIO), 1) // AUDIO
    video_first = jnp.concatenate([firsts[0:1]] * 2, axis=1)
    audio_first = jnp.concatenate([firsts[8:9]] * 4, axis=1)
    video_place = (audio_slot + window_start).astype(jnp.float32) - video_first
    audio_place = (video_slot + window_start).astype(jnp.float32) - audio_first
    cross_mask = jnp.where((video_place == 0.0) | (video_place == 1.0), 0.0, MASKED)
    audio_mask = jnp.where((audio_place == 0.0) | (audio_place == 1.0), 0.0, MASKED)
    return cross_mask, audio_mask


def softmax_and_grad(scaled, weight_grad):
    top = [jnp.max(s, axis=1, keepdims=True) for s in scaled]
    powers = [jnp.exp2(s - t) for s, t in zip(scaled, top)]
    scale = [1.0 / jnp.sum(p, axis=1, keepdims=True) for p in powers]
    weights = [p * s for p, s in zip(powers, scale)]
    rounded = [w.astype(jnp.bfloat16) for w in weights]
    row_dot = [
        jnp.sum(r.astype(jnp.float32) * g, axis=1, keepdims=True)
        for r, g in zip(rounded, weight_grad)
    ]
    score_grad = [
        (w * (g - d)).astype(jnp.bfloat16) for w, g, d in zip(weights, weight_grad, row_dot)
    ]
    return rounded, score_grad


def attention_kernel(
    last_group,
    group_ref,
    kv,
    qg,
    before_2,
    before_3,
    relayed_3,
    after,
    qg_out,
    kv_out,
    before_2_out,
    before_3_out,
    after_out,
    before_sum,
):
    group = group_ref[0]
    before_sum[...] = before_3[...] + relayed_3[...]
    members = range(MEMBERS)
    sources = [before_2, before_sum] + [kv.at[m] for m in members] + [after]
    targets = [before_2_out, before_3_out] + [kv_out.at[m] for m in members] + [after_out]
    bias_before = jnp.where(group == 0, MASKED, 0.0)
    bias_after = jnp.where(group == last_group, MASKED, 0.0)

    queries = [qg[m, 0:STACK] for m in members]
    cotangents = [qg[m, STACK:ROWS] for m in members]
    video_queries = [q[0:VIDEO] for q in queries]
    video_cotangents = [g[0:VIDEO] for g in cotangents]
    windows = [sources[m : m + WINDOW_BLOCKS] for m in members]
    keys = [jnp.concatenate([b[0:128] for b in w], axis=0) for w in windows]
    values = [jnp.concatenate([b[128:256] for b in w], axis=0) for w in windows]
    audio_keys = [jnp.concatenate([b[256:320] for b in w], axis=0) for w in windows]
    audio_values = [jnp.concatenate([b[320:384] for b in w], axis=0) for w in windows]

    rounded, score_grads, cross_rounded, cross_score_grads = [], [], [], []
    for m in members:
        cross_mask, audio_mask = masks_of(
            group * MEMBERS + m - HALF_WINDOW, qg[m, ROWS : ROWS + LIST_ROWS]
        )
        scaled = product(queries[m], keys[m], 1, 1) * LOG2_SCALE
        cross_scaled = product(video_queries[m], audio_keys[m], 1, 1) * LOG2_SCALE
        video_scaled = scaled[0:VIDEO]
        if m < HALF_WINDOW:
            split = (HALF_WINDOW - m) * VIDEO
            video_scaled = jnp.concatenate(
                [video_scaled[:, :split] + bias_before, video_scaled[:, split:]], axis=1
            )
        elif m == MEMBERS - 1:
            split = (WINDOW_BLOCKS - 1) * VIDEO
            video_scaled = jnp.concatenate(
                [video_scaled[:, :split], video_scaled[:, split:] + bias_after], axis=1
            )
        scaled = jnp.concatenate([video_scaled, scaled[VIDEO:STACK] + audio_mask], axis=0)
        weight_grad = product(cotangents[m], values[m], 1, 1)
        cross_grad = product(video_cotangents[m], audio_values[m], 1, 1)
        (r, cr), (s, cs) = softmax_and_grad(
            (scaled, cross_scaled + cross_mask), (weight_grad, cross_grad)
        )
        rounded.append(r)
        score_grads.append(s)
        cross_rounded.append(cr)
        cross_score_grads.append(cs)

    result = [product(rounded[m], values[m], 1, 0) for m in members]
    cross_result = [product(cross_rounded[m], audio_values[m], 1, 0) for m in members]
    query_term = [product(score_grads[m], keys[m], 1, 0) for m in members]
    cross_query = [product(cross_score_grads[m], audio_keys[m], 1, 0) for m in members]
    ak_terms = [product(cross_score_grads[m], video_queries[m], 0, 0) for m in members]
    av_terms = [product(cross_rounded[m], video_cotangents[m], 0, 0) for m in members]
    for m in members:
        qg_out[m, 0:128] = (result[m][0:VIDEO] + cross_result[m]).astype(jnp.bfloat16)
        qg_out[m, 128:192] = result[m][VIDEO:STACK].astype(jnp.bfloat16)
        qg_out[m, 192:320] = (
            (query_term[m][0:VIDEO] + cross_query[m]) * SCALE
        ).astype(jnp.bfloat16)
        qg_out[m, 320:384] = (query_term[m][VIDEO:STACK] * SCALE).astype(jnp.bfloat16)

    for block in range(EXTENDED):
        target = targets[block]
        users = [m for m in members if 0 <= block - m < WINDOW_BLOCKS]
        columns = {m: slice((block - m) * VIDEO, (block - m + 1) * VIDEO) for m in users}
        rows = {m: slice((block - m) * AUDIO, (block - m + 1) * AUDIO) for m in users}
        vk_sum = product(
            stacked([score_grads[m][:, columns[m]] for m in users]),
            stacked([queries[m] for m in users]),
            0,
            0,
        )
        vv_sum = product(
            stacked([rounded[m][:, columns[m]] for m in users]),
            stacked([cotangents[m] for m in users]),
            0,
            0,
        )
        ak_sum = sum(ak_terms[m][rows[m]] for m in users)
        av_sum = sum(av_terms[m][rows[m]] for m in users)
        target[0:128] = (vk_sum * SCALE).astype(target.dtype)
        target[128:256] = vv_sum.astype(target.dtype)
        target[256:320] = (ak_sum * SCALE).astype(target.dtype)
        target[320:384] = av_sum.astype(target.dtype)


def whole(memory=pltpu.VMEM):
    return pl.BlockSpec(memory_space=memory)


PACKED_KV = jax.ShapeDtypeStruct((MEMBERS, ROWS, GROUP_WIDTH), jnp.bfloat16)
BLOCK_KV = jax.ShapeDtypeStruct((ROWS, GROUP_WIDTH), jnp.bfloat16)
PACKED_QG = jax.ShapeDtypeStruct((MEMBERS, ROWS + LIST_ROWS, GROUP_WIDTH), jnp.bfloat16)


def pack_kv(shift, *arrays):
    return pl.pallas_call(
        pack_kv_kernel,
        out_shape=PACKED_KV,
        in_specs=[whole(pltpu.SMEM)] + [whole(pl.ANY)] * 4,
        out_specs=whole(),
        scratch_shapes=[pltpu.SemaphoreType.DMA((MEMBERS, 4))],
        compiler_params=LARGE,
        name="pack_kv",
    )(shift, *arrays)


def pack_qg(shift, *arrays):
    return pl.pallas_call(
        pack_qg_kernel,
        out_shape=PACKED_QG,
        in_specs=[whole(pltpu.SMEM)] * 3 + [whole(pl.ANY)] * 4,
        out_specs=whole(),
        scratch_shapes=[pltpu.SemaphoreType.DMA((MEMBERS, 4))],
        compiler_params=LARGE,
        name="pack_qg",
    )(shift, *arrays)


def unpack(kernel, rows, *arrays):
    scalars = sum(array.dtype == jnp.int32 for array in arrays)
    return pl.pallas_call(
        kernel,
        out_shape=[jax.ShapeDtypeStruct((r, HEADS * HEAD_SIZE), jnp.bfloat16) for r in rows],
        in_specs=[whole(pltpu.SMEM)] * scalars + [whole()] * (len(arrays) - scalars),
        out_specs=[whole()] * len(rows),
        compiler_params=SMALL,
        name="unpack",
    )(*arrays)


def merge(groups, *arrays):
    return pl.pallas_call(
        functools.partial(merge_kernel, groups - 1),
        out_shape=[BLOCK_KV] * MEMBERS,
        in_specs=[whole(pltpu.SMEM)] * 2 + [whole()] * 5,
        out_specs=[whole()] * MEMBERS,
        scratch_shapes=[pltpu.VMEM((MEMBERS, ROWS, GROUP_WIDTH), jnp.bfloat16)],
        compiler_params=SMALL,
        name="merge",
    )(*arrays)


def attention(groups, group, *arrays):
    def head_block(*leading):
        zeros = (0,) * len(leading)
        return pl.BlockSpec(leading + (HEAD_SIZE,), lambda head: zeros + (head,))

    return pl.pallas_call(
        functools.partial(attention_kernel, groups - 1),
        grid=(GROUP_HEADS,),
        out_shape=[PACKED_KV] * 2 + [BLOCK_KV] * 3,
        in_specs=[
            whole(pltpu.SMEM),
            head_block(MEMBERS, ROWS),
            head_block(MEMBERS, ROWS + LIST_ROWS),
            *[head_block(ROWS)] * 4,
        ],
        out_specs=[head_block(MEMBERS, ROWS)] * 2 + [head_block(ROWS)] * 3,
        scratch_shapes=[pltpu.VMEM((ROWS, HEAD_SIZE), jnp.bfloat16)],
        compiler_params=LARGE,
        name="attention",
    )(group, *arrays)


def slice_shift():
    clip, tower = lax.axis_index("clip"), lax.axis_index("tower")
    shifted = (clip == lax.axis_size("clip") - 1) & (tower == 1)
    return jnp.where(shifted, 1, 0).astype(jnp.int32).reshape(1)


def moved(block, hops):
    clips, towers = lax.axis_size("clip"), lax.axis_size("tower")
    per_tower = lax.axis_size("group")
    route = []
    for clip in range(clips):
        for group, target in hops:
            turn = target // per_tower - group // per_tower if clip == clips - 1 else 0
            for member in range(MEMBERS):
                route.append(
                    (
                        (clip * towers * per_tower + group) * MEMBERS + member,
                        (clip * towers * per_tower + target) * MEMBERS
                        + (member - turn) % MEMBERS,
                    )
                )
    return lax.ppermute(block, ("clip", "tower", "group", "member"), route)


def to_group(block, distance):
    groups = lax.axis_size(("tower", "group"))
    hops = [(g, g + distance) for g in range(groups) if 0 <= g + distance < groups]
    return moved(block, hops)


def to_group_by_relay(block, distance):
    groups, per_tower = lax.axis_size(("tower", "group")), lax.axis_size("group")
    relay = 0 if distance > 0 else groups - 1
    first, second = [], []
    for group in range(groups):
        target = group + distance
        if not 0 <= target < groups:
            continue
        if group // per_tower == target // per_tower:
            first.append((group, target))
        else:
            first.append((group, relay))
            second.append((relay, target))
    arrived = moved(block, first)
    return arrived, moved(arrived, second)


def exchange(packed):
    return lax.all_to_all(packed, "member", 0, 0)


def send_round(blocks):
    return [blocks[0]] + [
        lax.ppermute(blocks[d], "member", [(i, (i + d) % MEMBERS) for i in range(MEMBERS)])
        for d in range(1, MEMBERS)
    ]


def body(
    video_query,
    video_keys,
    video_value,
    audio_query,
    audio_key,
    audio_value,
    video_cotangent,
    audio_cotangent,
    video_lists,
    audio_lists,
):
    groups = lax.axis_size(("tower", "group"))
    group = lax.axis_index(("tower", "group")).astype(jnp.int32).reshape(1)
    shift = slice_shift()
    me = lax.axis_index("member").astype(jnp.int32).reshape(1)
    kv_packed = pack_kv(shift, video_keys, video_value, audio_key, audio_value)
    kv = exchange(kv_packed)
    qg_packed = pack_qg(
        shift,
        video_lists,
        audio_lists,
        video_query,
        audio_query,
        video_cotangent,
        audio_cotangent,
    )
    before_3, relayed_3 = to_group_by_relay(kv[3], 1)
    before_2 = to_group(kv[2], 1)
    after = to_group(kv[0], -1)
    qg = exchange(qg_packed)
    qg_part, kv_part, part_2, part_3, after_part = attention(
        groups, group, kv, qg, before_2, before_3, relayed_3, after
    )
    qg_back = exchange(qg_part)
    from_after_3, relayed_back = to_group_by_relay(part_3, -1)
    from_after_2 = to_group(part_2, -1)
    from_before = to_group(after_part, 1)
    kvs_back = send_round(
        merge(
            groups,
            group,
            me,
            kv_part,
            from_after_2,
            from_after_3,
            relayed_back,
            from_before,
        )
    )
    video_output, audio_output, video_query_grad, audio_query_grad = unpack(
        unpack_qg_kernel, (VIDEO, AUDIO, VIDEO, AUDIO), shift, qg_back
    )
    video_key_grad, video_value_grad, audio_key_grad, audio_value_grad = unpack(
        unpack_kv_kernel, (VIDEO, VIDEO, AUDIO, AUDIO), shift, me, *kvs_back
    )
    return (
        video_output,
        audio_output,
        video_query_grad,
        video_key_grad,
        video_value_grad,
        audio_query_grad,
        audio_key_grad,
        audio_value_grad,
    )


def solution(mesh):
    shape = mesh.devices.shape
    fine = Mesh(
        mesh.devices.reshape(shape[0], shape[1], shape[2] // MEMBERS, MEMBERS),
        ("clip", "tower", "group", "member"),
    )
    placed = P(("clip", "tower", "group", "member"), None)
    return jax.shard_map(
        body,
        mesh=fine,
        in_specs=(placed,) * 10,
        out_specs=(placed,) * 8,
        check_vma=False,
    )
```

```python
import functools

import jax
import jax.numpy as jnp
from jax import lax
from jax.experimental import pallas as pl
from jax.experimental.pallas import tpu as pltpu
from jax.sharding import Mesh
from jax.sharding import PartitionSpec as P

HEADS = 12
HEAD_SIZE = 128
WINDOW_BLOCKS = 4
HALF_WINDOW = 2
MEMBERS = 4
DISTANCES = (0, 2, 1, 3)
GROUP_HEADS = HEADS // MEMBERS
GROUP_WIDTH = GROUP_HEADS * HEAD_SIZE
EXTENDED = MEMBERS + WINDOW_BLOCKS - 1
VIDEO = 128
AUDIO = 64
STACK = VIDEO + AUDIO
ROWS = 2 * STACK
LIST_ROWS = 16
SCALE = HEAD_SIZE ** -0.5
LOG2_SCALE = SCALE * 1.4426950408889634
MASKED = -1e30
LARGE = pltpu.CompilerParams(vmem_limit_bytes=60 * 1024 * 1024)
SMALL = pltpu.CompilerParams(vmem_limit_bytes=16 * 1024 * 1024)


def product(left, right, left_dim, right_dim):
    return lax.dot_general(
        left,
        right,
        (((left_dim,), (right_dim,)), ((), ())),
        preferred_element_type=jnp.float32,
    )


def start_packing(copies, sems, first, arrays, target):
    columns = pl.ds(pl.multiple_of(first, GROUP_WIDTH), GROUP_WIDTH)
    row = 0
    for index, array in enumerate(arrays):
        rows = array.shape[0]
        copy = pltpu.make_async_copy(
            array.at[:, columns], target.at[row : row + rows], sems.at[index]
        )
        copy.start()
        copies.append(copy)
        row += rows


def pack_kv_kernel(shift, vk, vv, ak, av, out, sems):
    copies = []
    for member in range(MEMBERS):
        first = lax.rem(shift[0] + member, MEMBERS) * GROUP_WIDTH
        start_packing(copies, sems.at[member], first, (vk, vv, ak, av), out.at[member])
    for copy in copies:
        copy.wait()


def pack_qg_kernel(shift, video_list, audio_list, vq, aq, vg, ag, out, sems):
    copies = []
    for member in range(MEMBERS):
        first = lax.rem(shift[0] + member, MEMBERS) * GROUP_WIDTH
        start_packing(copies, sems.at[member], first, (vq, aq, vg, ag), out.at[member])
    video_first = jnp.full((8, GROUP_WIDTH), video_list[0, 0].astype(jnp.float32))
    audio_first = jnp.full((8, GROUP_WIDTH), audio_list[0, 0].astype(jnp.float32))
    firsts = jnp.concatenate([video_first, audio_first], axis=0).astype(jnp.bfloat16)
    for member in range(MEMBERS):
        out[member, ROWS : ROWS + LIST_ROWS] = firsts
    for copy in copies:
        copy.wait()


def unpack_rows(packed, columns, outs):
    row = 0
    for out in outs:
        rows = out.shape[0]
        out[:, columns] = packed[row : row + rows]
        row += rows


def columns_of(member):
    first = lax.rem(member, MEMBERS) * GROUP_WIDTH
    return pl.ds(pl.multiple_of(first, GROUP_WIDTH), GROUP_WIDTH)


def unpack_qg_kernel(shift, packed, *outs):
    for member in range(MEMBERS):
        unpack_rows(packed.at[member], columns_of(shift[0] + member), outs)


def unpack_kv_kernel(shift, me, *refs):
    blocks, outs = refs[:MEMBERS], refs[MEMBERS:]
    for distance, block in zip(DISTANCES, blocks):
        unpack_rows(block, columns_of(shift[0] + me[0] + MEMBERS - distance), outs)


def merge_kernel(
    last_group, group_ref, me, own, from_after_2, from_after_3, relayed_3, from_before, *refs
):
    outs, out = refs[:MEMBERS], refs[MEMBERS]

    def total(member, *received):
        parts = [own[member].astype(jnp.float32)]
        parts += [r[...].astype(jnp.float32) for r in received]
        out[member] = sum(parts).astype(jnp.bfloat16)

    total(0, from_before)
    out[1] = own[1]
    total(2, from_after_2)
    total(3, relayed_3)

    @pl.when(group_ref[0] != last_group)
    def _():
        total(3, from_after_3, relayed_3)

    for distance, target in enumerate(outs):
        target[...] = out[lax.rem(me[0] + distance, MEMBERS)]


def stacked(parts):
    return parts[0] if len(parts) == 1 else jnp.concatenate(parts, axis=0)


def masks_of(window_start, firsts):
    firsts = firsts.astype(jnp.float32)
    video_slot = lax.broadcasted_iota(jnp.int32, (1, WINDOW_BLOCKS * VIDEO), 1) // VIDEO
    audio_slot = lax.broadcasted_iota(jnp.int32, (1, WINDOW_BLOCKS * AUDIO), 1) // AUDIO
    video_first = jnp.concatenate([firsts[0:1]] * 2, axis=1)
    audio_first = jnp.concatenate([firsts[8:9]] * 4, axis=1)
    video_place = (audio_slot + window_start).astype(jnp.float32) - video_first
    audio_place = (video_slot + window_start).astype(jnp.float32) - audio_first
    cross_mask = jnp.where((video_place == 0.0) | (video_place == 1.0), 0.0, MASKED)
    audio_mask = jnp.where((audio_place == 0.0) | (audio_place == 1.0), 0.0, MASKED)
    return cross_mask, audio_mask


def softmax_and_grad(scaled, weight_grad):
    top = [jnp.max(s, axis=1, keepdims=True) for s in scaled]
    powers = [jnp.exp2(s - t) for s, t in zip(scaled, top)]
    scale = [1.0 / jnp.sum(p, axis=1, keepdims=True) for p in powers]
    weights = [p * s for p, s in zip(powers, scale)]
    rounded = [w.astype(jnp.bfloat16) for w in weights]
    row_dot = [
        jnp.sum(r.astype(jnp.float32) * g, axis=1, keepdims=True)
        for r, g in zip(rounded, weight_grad)
    ]
    score_grad = [
        (w * (g - d)).astype(jnp.bfloat16) for w, g, d in zip(weights, weight_grad, row_dot)
    ]
    return rounded, score_grad


def attention_kernel(
    last_group,
    group_ref,
    kv,
    qg,
    before_2,
    before_3,
    relayed_3,
    after,
    qg_out,
    kv_out,
    before_2_out,
    before_3_out,
    after_out,
    before_sum,
):
    group = group_ref[0]
    before_sum[...] = before_3[...] + relayed_3[...]
    members = range(MEMBERS)
    sources = [before_2, before_sum] + [kv.at[m] for m in members] + [after]
    targets = [before_2_out, before_3_out] + [kv_out.at[m] for m in members] + [after_out]
    bias_before = jnp.where(group == 0, MASKED, 0.0)
    bias_after = jnp.where(group == last_group, MASKED, 0.0)

    queries = [qg[m, 0:STACK] for m in members]
    cotangents = [qg[m, STACK:ROWS] for m in members]
    video_queries = [q[0:VIDEO] for q in queries]
    video_cotangents = [g[0:VIDEO] for g in cotangents]
    windows = [sources[m : m + WINDOW_BLOCKS] for m in members]
    keys = [jnp.concatenate([b[0:128] for b in w], axis=0) for w in windows]
    values = [jnp.concatenate([b[128:256] for b in w], axis=0) for w in windows]
    audio_keys = [jnp.concatenate([b[256:320] for b in w], axis=0) for w in windows]
    audio_values = [jnp.concatenate([b[320:384] for b in w], axis=0) for w in windows]

    rounded, score_grads, cross_rounded, cross_score_grads = [], [], [], []
    for m in members:
        cross_mask, audio_mask = masks_of(
            group * MEMBERS + m - HALF_WINDOW, qg[m, ROWS : ROWS + LIST_ROWS]
        )
        scaled = product(queries[m], keys[m], 1, 1) * LOG2_SCALE
        cross_scaled = product(video_queries[m], audio_keys[m], 1, 1) * LOG2_SCALE
        video_scaled = scaled[0:VIDEO]
        if m < HALF_WINDOW:
            split = (HALF_WINDOW - m) * VIDEO
            video_scaled = jnp.concatenate(
                [video_scaled[:, :split] + bias_before, video_scaled[:, split:]], axis=1
            )
        elif m == MEMBERS - 1:
            split = (WINDOW_BLOCKS - 1) * VIDEO
            video_scaled = jnp.concatenate(
                [video_scaled[:, :split], video_scaled[:, split:] + bias_after], axis=1
            )
        scaled = jnp.concatenate([video_scaled, scaled[VIDEO:STACK] + audio_mask], axis=0)
        weight_grad = product(cotangents[m], values[m], 1, 1)
        cross_grad = product(video_cotangents[m], audio_values[m], 1, 1)
        (r, cr), (s, cs) = softmax_and_grad(
            (scaled, cross_scaled + cross_mask), (weight_grad, cross_grad)
        )
        rounded.append(r)
        score_grads.append(s)
        cross_rounded.append(cr)
        cross_score_grads.append(cs)

    result = [product(rounded[m], values[m], 1, 0) for m in members]
    cross_result = [product(cross_rounded[m], audio_values[m], 1, 0) for m in members]
    query_term = [product(score_grads[m], keys[m], 1, 0) for m in members]
    cross_query = [product(cross_score_grads[m], audio_keys[m], 1, 0) for m in members]
    ak_terms = [product(cross_score_grads[m], video_queries[m], 0, 0) for m in members]
    av_terms = [product(cross_rounded[m], video_cotangents[m], 0, 0) for m in members]
    for m in members:
        qg_out[m, 0:128] = (result[m][0:VIDEO] + cross_result[m]).astype(jnp.bfloat16)
        qg_out[m, 128:192] = result[m][VIDEO:STACK].astype(jnp.bfloat16)
        qg_out[m, 192:320] = (
            (query_term[m][0:VIDEO] + cross_query[m]) * SCALE
        ).astype(jnp.bfloat16)
        qg_out[m, 320:384] = (query_term[m][VIDEO:STACK] * SCALE).astype(jnp.bfloat16)

    for block in range(EXTENDED):
        target = targets[block]
        users = [m for m in members if 0 <= block - m < WINDOW_BLOCKS]
        columns = {m: slice((block - m) * VIDEO, (block - m + 1) * VIDEO) for m in users}
        rows = {m: slice((block - m) * AUDIO, (block - m + 1) * AUDIO) for m in users}
        vk_sum = product(
            stacked([score_grads[m][:, columns[m]] for m in users]),
            stacked([queries[m] for m in users]),
            0,
            0,
        )
        vv_sum = product(
            stacked([rounded[m][:, columns[m]] for m in users]),
            stacked([cotangents[m] for m in users]),
            0,
            0,
        )
        ak_sum = sum(ak_terms[m][rows[m]] for m in users)
        av_sum = sum(av_terms[m][rows[m]] for m in users)
        target[0:128] = (vk_sum * SCALE).astype(target.dtype)
        target[128:256] = vv_sum.astype(target.dtype)
        target[256:320] = (ak_sum * SCALE).astype(target.dtype)
        target[320:384] = av_sum.astype(target.dtype)


def whole(memory=pltpu.VMEM):
    return pl.BlockSpec(memory_space=memory)


PACKED_KV = jax.ShapeDtypeStruct((MEMBERS, ROWS, GROUP_WIDTH), jnp.bfloat16)
BLOCK_KV = jax.ShapeDtypeStruct((ROWS, GROUP_WIDTH), jnp.bfloat16)
PACKED_QG = jax.ShapeDtypeStruct((MEMBERS, ROWS + LIST_ROWS, GROUP_WIDTH), jnp.bfloat16)


def pack_kv(shift, *arrays):
    return pl.pallas_call(
        pack_kv_kernel,
        out_shape=PACKED_KV,
        in_specs=[whole(pltpu.SMEM)] + [whole(pl.ANY)] * 4,
        out_specs=whole(),
        scratch_shapes=[pltpu.SemaphoreType.DMA((MEMBERS, 4))],
        compiler_params=LARGE,
        name="pack_kv",
    )(shift, *arrays)


def pack_qg(shift, *arrays):
    return pl.pallas_call(
        pack_qg_kernel,
        out_shape=PACKED_QG,
        in_specs=[whole(pltpu.SMEM)] * 3 + [whole(pl.ANY)] * 4,
        out_specs=whole(),
        scratch_shapes=[pltpu.SemaphoreType.DMA((MEMBERS, 4))],
        compiler_params=LARGE,
        name="pack_qg",
    )(shift, *arrays)


def unpack(kernel, rows, *arrays):
    scalars = sum(array.dtype == jnp.int32 for array in arrays)
    return pl.pallas_call(
        kernel,
        out_shape=[jax.ShapeDtypeStruct((r, HEADS * HEAD_SIZE), jnp.bfloat16) for r in rows],
        in_specs=[whole(pltpu.SMEM)] * scalars + [whole()] * (len(arrays) - scalars),
        out_specs=[whole()] * len(rows),
        compiler_params=SMALL,
        name="unpack",
    )(*arrays)


def merge(groups, *arrays):
    return pl.pallas_call(
        functools.partial(merge_kernel, groups - 1),
        out_shape=[BLOCK_KV] * MEMBERS,
        in_specs=[whole(pltpu.SMEM)] * 2 + [whole()] * 5,
        out_specs=[whole()] * MEMBERS,
        scratch_shapes=[pltpu.VMEM((MEMBERS, ROWS, GROUP_WIDTH), jnp.bfloat16)],
        compiler_params=SMALL,
        name="merge",
    )(*arrays)


def attention(groups, group, *arrays):
    def head_block(*leading):
        zeros = (0,) * len(leading)
        return pl.BlockSpec(leading + (HEAD_SIZE,), lambda head: zeros + (head,))

    return pl.pallas_call(
        functools.partial(attention_kernel, groups - 1),
        grid=(GROUP_HEADS,),
        out_shape=[PACKED_KV] * 2 + [BLOCK_KV] * 3,
        in_specs=[
            whole(pltpu.SMEM),
            head_block(MEMBERS, ROWS),
            head_block(MEMBERS, ROWS + LIST_ROWS),
            *[head_block(ROWS)] * 4,
        ],
        out_specs=[head_block(MEMBERS, ROWS)] * 2 + [head_block(ROWS)] * 3,
        scratch_shapes=[pltpu.VMEM((ROWS, HEAD_SIZE), jnp.bfloat16)],
        compiler_params=LARGE,
        name="attention",
    )(group, *arrays)


def slice_shift():
    clip, tower = lax.axis_index("clip"), lax.axis_index("tower")
    shifted = (clip == lax.axis_size("clip") - 1) & (tower == 1)
    return jnp.where(shifted, 1, 0).astype(jnp.int32).reshape(1)


def moved(block, hops):
    clips, towers = lax.axis_size("clip"), lax.axis_size("tower")
    per_tower = lax.axis_size("group")
    route = []
    for clip in range(clips):
        for group, target in hops:
            turn = target // per_tower - group // per_tower if clip == clips - 1 else 0
            for member in range(MEMBERS):
                route.append(
                    (
                        (clip * towers * per_tower + group) * MEMBERS + member,
                        (clip * towers * per_tower + target) * MEMBERS
                        + (member - turn) % MEMBERS,
                    )
                )
    return lax.ppermute(block, ("clip", "tower", "group", "member"), route)


def to_group(block, distance):
    groups = lax.axis_size(("tower", "group"))
    hops = [(g, g + distance) for g in range(groups) if 0 <= g + distance < groups]
    return moved(block, hops)


def to_group_by_relay(block, distance):
    groups, per_tower = lax.axis_size(("tower", "group")), lax.axis_size("group")
    relay = 0 if distance > 0 else groups - 1
    first, second = [], []
    for group in range(groups):
        target = group + distance
        if not 0 <= target < groups:
            continue
        if group // per_tower == target // per_tower:
            first.append((group, target))
        else:
            first.append((group, relay))
            second.append((relay, target))
    arrived = moved(block, first)
    return arrived, moved(arrived, second)


def exchange(packed):
    return lax.all_to_all(packed, "member", 0, 0)


def send_round(blocks):
    received = {0: blocks[0]}
    for d in range(1, MEMBERS):
        route = [(i, (i + d) % MEMBERS) for i in range(MEMBERS)]
        received[d] = lax.ppermute(blocks[d], "member", route)
    return [received[d] for d in DISTANCES]


def body(
    video_query,
    video_keys,
    video_value,
    audio_query,
    audio_key,
    audio_value,
    video_cotangent,
    audio_cotangent,
    video_lists,
    audio_lists,
):
    groups = lax.axis_size(("tower", "group"))
    group = lax.axis_index(("tower", "group")).astype(jnp.int32).reshape(1)
    shift = slice_shift()
    me = lax.axis_index("member").astype(jnp.int32).reshape(1)
    kv_packed = pack_kv(shift, video_keys, video_value, audio_key, audio_value)
    kv = exchange(kv_packed)
    qg_packed = pack_qg(
        shift,
        video_lists,
        audio_lists,
        video_query,
        audio_query,
        video_cotangent,
        audio_cotangent,
    )
    before_3, relayed_3 = to_group_by_relay(kv[3], 1)
    before_2 = to_group(kv[2], 1)
    after = to_group(kv[0], -1)
    qg = exchange(qg_packed)
    qg_part, kv_part, part_2, part_3, after_part = attention(
        groups, group, kv, qg, before_2, before_3, relayed_3, after
    )
    qg_back = exchange(qg_part)
    from_after_3, relayed_back = to_group_by_relay(part_3, -1)
    from_after_2 = to_group(part_2, -1)
    from_before = to_group(after_part, 1)
    kvs_back = send_round(
        merge(
            groups,
            group,
            me,
            kv_part,
            from_after_2,
            from_after_3,
            relayed_back,
            from_before,
        )
    )
    video_output, audio_output, video_query_grad, audio_query_grad = unpack(
        unpack_qg_kernel, (VIDEO, AUDIO, VIDEO, AUDIO), shift, qg_back
    )
    video_key_grad, video_value_grad, audio_key_grad, audio_value_grad = unpack(
        unpack_kv_kernel, (VIDEO, VIDEO, AUDIO, AUDIO), shift, me, *kvs_back
    )
    return (
        video_output,
        audio_output,
        video_query_grad,
        video_key_grad,
        video_value_grad,
        audio_query_grad,
        audio_key_grad,
        audio_value_grad,
    )


def solution(mesh):
    shape = mesh.devices.shape
    fine = Mesh(
        mesh.devices.reshape(shape[0], shape[1], shape[2] // MEMBERS, MEMBERS),
        ("clip", "tower", "group", "member"),
    )
    placed = P(("clip", "tower", "group", "member"), None)
    return jax.shard_map(
        body,
        mesh=fine,
        in_specs=(placed,) * 10,
        out_specs=(placed,) * 8,
        check_vma=False,
    )
```

```python
import functools

import jax
import jax.numpy as jnp
from jax import lax
from jax.experimental import pallas as pl
from jax.experimental.pallas import tpu as pltpu
from jax.sharding import Mesh
from jax.sharding import PartitionSpec as P

HEADS = 12
HEAD_SIZE = 128
WINDOW_BLOCKS = 4
HALF_WINDOW = 2
MEMBERS = 4
DISTANCES = (0, 2, 1, 3)
GROUP_HEADS = HEADS // MEMBERS
GROUP_WIDTH = GROUP_HEADS * HEAD_SIZE
EXTENDED = MEMBERS + WINDOW_BLOCKS - 1
VIDEO = 128
AUDIO = 64
STACK = VIDEO + AUDIO
ROWS = 2 * STACK
SCALE = HEAD_SIZE ** -0.5
LOG2_SCALE = SCALE * 1.4426950408889634
MASKED = -1e30
LARGE = pltpu.CompilerParams(vmem_limit_bytes=60 * 1024 * 1024)
SMALL = pltpu.CompilerParams(vmem_limit_bytes=16 * 1024 * 1024)


def product(left, right, left_dim, right_dim):
    return lax.dot_general(
        left,
        right,
        (((left_dim,), (right_dim,)), ((), ())),
        preferred_element_type=jnp.float32,
    )


def start_packing(copies, sems, first, arrays, target):
    columns = pl.ds(pl.multiple_of(first, GROUP_WIDTH), GROUP_WIDTH)
    row = 0
    for index, array in enumerate(arrays):
        rows = array.shape[0]
        copy = pltpu.make_async_copy(
            array.at[:, columns], target.at[row : row + rows], sems.at[index]
        )
        copy.start()
        copies.append(copy)
        row += rows


def pack_kv_kernel(shift, vk, vv, ak, av, out, sems):
    copies = []
    for member in range(MEMBERS):
        first = lax.rem(shift[0] + member, MEMBERS) * GROUP_WIDTH
        start_packing(copies, sems.at[member], first, (vk, vv, ak, av), out.at[member])
    for copy in copies:
        copy.wait()


def pack_qg_kernel(shift, vq, aq, vg, ag, out, sems):
    copies = []
    for member in range(MEMBERS):
        first = lax.rem(shift[0] + member, MEMBERS) * GROUP_WIDTH
        start_packing(copies, sems.at[member], first, (vq, aq, vg, ag), out.at[member])
    for copy in copies:
        copy.wait()


def unpack_rows(packed, columns, outs):
    row = 0
    for out in outs:
        rows = out.shape[0]
        out[:, columns] = packed[row : row + rows]
        row += rows


def columns_of(member):
    first = lax.rem(member, MEMBERS) * GROUP_WIDTH
    return pl.ds(pl.multiple_of(first, GROUP_WIDTH), GROUP_WIDTH)


def unpack_qg_kernel(shift, packed, *outs):
    for member in range(MEMBERS):
        unpack_rows(packed.at[member], columns_of(shift[0] + member), outs)


def unpack_kv_kernel(shift, me, *refs):
    blocks, outs = refs[:MEMBERS], refs[MEMBERS:]
    for distance, block in zip(DISTANCES, blocks):
        unpack_rows(block, columns_of(shift[0] + me[0] + MEMBERS - distance), outs)


def merge_kernel(
    last_group, group_ref, me, own, from_after_2, from_after_3, relayed_3, from_before, *refs
):
    outs, out = refs[:MEMBERS], refs[MEMBERS]

    def total(member, *received):
        parts = [own[member].astype(jnp.float32)]
        parts += [r[...].astype(jnp.float32) for r in received]
        out[member] = sum(parts).astype(jnp.bfloat16)

    total(0, from_before)
    out[1] = own[1]
    total(2, from_after_2)
    total(3, relayed_3)

    @pl.when(group_ref[0] != last_group)
    def _():
        total(3, from_after_3, relayed_3)

    for distance, target in enumerate(outs):
        target[...] = out[lax.rem(me[0] + distance, MEMBERS)]


def stacked(parts):
    return parts[0] if len(parts) == 1 else jnp.concatenate(parts, axis=0)


def masks_of(window_start, video_first, audio_first):
    video_slot = lax.broadcasted_iota(jnp.int32, (1, WINDOW_BLOCKS * VIDEO), 1) // VIDEO
    audio_slot = lax.broadcasted_iota(jnp.int32, (1, WINDOW_BLOCKS * AUDIO), 1) // AUDIO
    video_place = audio_slot + window_start - video_first
    audio_place = video_slot + window_start - audio_first
    cross_mask = jnp.where((video_place == 0) | (video_place == 1), 0.0, MASKED)
    audio_mask = jnp.where((audio_place == 0) | (audio_place == 1), 0.0, MASKED)
    return cross_mask, audio_mask


def softmax_and_grad(scaled, weight_grad):
    top = [jnp.max(s, axis=1, keepdims=True) for s in scaled]
    powers = [jnp.exp2(s - t) for s, t in zip(scaled, top)]
    scale = [1.0 / jnp.sum(p, axis=1, keepdims=True) for p in powers]
    weights = [p * s for p, s in zip(powers, scale)]
    rounded = [w.astype(jnp.bfloat16) for w in weights]
    row_dot = [
        jnp.sum(r.astype(jnp.float32) * g, axis=1, keepdims=True)
        for r, g in zip(rounded, weight_grad)
    ]
    score_grad = [
        (w * (g - d)).astype(jnp.bfloat16) for w, g, d in zip(weights, weight_grad, row_dot)
    ]
    return rounded, score_grad


def attention_kernel(
    last_group,
    group_ref,
    firsts,
    kv,
    qg,
    before_2,
    before_3,
    relayed_3,
    after,
    qg_out,
    kv_out,
    before_2_out,
    before_3_out,
    after_out,
    before_sum,
):
    group = group_ref[0]
    before_sum[...] = before_3[...] + relayed_3[...]
    members = range(MEMBERS)
    sources = [before_2, before_sum] + [kv.at[m] for m in members] + [after]
    targets = [before_2_out, before_3_out] + [kv_out.at[m] for m in members] + [after_out]
    bias_before = jnp.where(group == 0, MASKED, 0.0)
    bias_after = jnp.where(group == last_group, MASKED, 0.0)

    queries = [qg[m, 0:STACK] for m in members]
    cotangents = [qg[m, STACK:ROWS] for m in members]
    video_queries = [q[0:VIDEO] for q in queries]
    video_cotangents = [g[0:VIDEO] for g in cotangents]
    windows = [sources[m : m + WINDOW_BLOCKS] for m in members]
    keys = [jnp.concatenate([b[0:128] for b in w], axis=0) for w in windows]
    values = [jnp.concatenate([b[128:256] for b in w], axis=0) for w in windows]
    audio_keys = [jnp.concatenate([b[256:320] for b in w], axis=0) for w in windows]
    audio_values = [jnp.concatenate([b[320:384] for b in w], axis=0) for w in windows]

    rounded, score_grads, cross_rounded, cross_score_grads = [], [], [], []
    for m in members:
        cross_mask, audio_mask = masks_of(
            group * MEMBERS + m - HALF_WINDOW, firsts[m, 0], firsts[m, 1]
        )
        scaled = product(queries[m], keys[m], 1, 1) * LOG2_SCALE
        cross_scaled = product(video_queries[m], audio_keys[m], 1, 1) * LOG2_SCALE
        video_scaled = scaled[0:VIDEO]
        if m < HALF_WINDOW:
            split = (HALF_WINDOW - m) * VIDEO
            video_scaled = jnp.concatenate(
                [video_scaled[:, :split] + bias_before, video_scaled[:, split:]], axis=1
            )
        elif m == MEMBERS - 1:
            split = (WINDOW_BLOCKS - 1) * VIDEO
            video_scaled = jnp.concatenate(
                [video_scaled[:, :split], video_scaled[:, split:] + bias_after], axis=1
            )
        scaled = jnp.concatenate([video_scaled, scaled[VIDEO:STACK] + audio_mask], axis=0)
        weight_grad = product(cotangents[m], values[m], 1, 1)
        cross_grad = product(video_cotangents[m], audio_values[m], 1, 1)
        (r, cr), (s, cs) = softmax_and_grad(
            (scaled, cross_scaled + cross_mask), (weight_grad, cross_grad)
        )
        rounded.append(r)
        score_grads.append(s)
        cross_rounded.append(cr)
        cross_score_grads.append(cs)

    result = [product(rounded[m], values[m], 1, 0) for m in members]
    cross_result = [product(cross_rounded[m], audio_values[m], 1, 0) for m in members]
    query_term = [product(score_grads[m], keys[m], 1, 0) for m in members]
    cross_query = [product(cross_score_grads[m], audio_keys[m], 1, 0) for m in members]
    ak_terms = [product(cross_score_grads[m], video_queries[m], 0, 0) for m in members]
    av_terms = [product(cross_rounded[m], video_cotangents[m], 0, 0) for m in members]
    for m in members:
        qg_out[m, 0:128] = (result[m][0:VIDEO] + cross_result[m]).astype(jnp.bfloat16)
        qg_out[m, 128:192] = result[m][VIDEO:STACK].astype(jnp.bfloat16)
        qg_out[m, 192:320] = (
            (query_term[m][0:VIDEO] + cross_query[m]) * SCALE
        ).astype(jnp.bfloat16)
        qg_out[m, 320:384] = (query_term[m][VIDEO:STACK] * SCALE).astype(jnp.bfloat16)

    for block in range(EXTENDED):
        target = targets[block]
        users = [m for m in members if 0 <= block - m < WINDOW_BLOCKS]
        columns = {m: slice((block - m) * VIDEO, (block - m + 1) * VIDEO) for m in users}
        rows = {m: slice((block - m) * AUDIO, (block - m + 1) * AUDIO) for m in users}
        vk_sum = product(
            stacked([score_grads[m][:, columns[m]] for m in users]),
            stacked([queries[m] for m in users]),
            0,
            0,
        )
        vv_sum = product(
            stacked([rounded[m][:, columns[m]] for m in users]),
            stacked([cotangents[m] for m in users]),
            0,
            0,
        )
        ak_sum = sum(ak_terms[m][rows[m]] for m in users)
        av_sum = sum(av_terms[m][rows[m]] for m in users)
        target[0:128] = (vk_sum * SCALE).astype(target.dtype)
        target[128:256] = vv_sum.astype(target.dtype)
        target[256:320] = (ak_sum * SCALE).astype(target.dtype)
        target[320:384] = av_sum.astype(target.dtype)


def whole(memory=pltpu.VMEM):
    return pl.BlockSpec(memory_space=memory)


PACKED_KV = jax.ShapeDtypeStruct((MEMBERS, ROWS, GROUP_WIDTH), jnp.bfloat16)
BLOCK_KV = jax.ShapeDtypeStruct((ROWS, GROUP_WIDTH), jnp.bfloat16)
def pack_kv(shift, *arrays):
    return pl.pallas_call(
        pack_kv_kernel,
        out_shape=PACKED_KV,
        in_specs=[whole(pltpu.SMEM)] + [whole(pl.ANY)] * 4,
        out_specs=whole(),
        scratch_shapes=[pltpu.SemaphoreType.DMA((MEMBERS, 4))],
        compiler_params=LARGE,
        name="pack_kv",
    )(shift, *arrays)


def pack_qg(shift, *arrays):
    return pl.pallas_call(
        pack_qg_kernel,
        out_shape=PACKED_KV,
        in_specs=[whole(pltpu.SMEM)] + [whole(pl.ANY)] * 4,
        out_specs=whole(),
        scratch_shapes=[pltpu.SemaphoreType.DMA((MEMBERS, 4))],
        compiler_params=LARGE,
        name="pack_qg",
    )(shift, *arrays)


def unpack(kernel, rows, *arrays):
    scalars = sum(array.dtype == jnp.int32 for array in arrays)
    return pl.pallas_call(
        kernel,
        out_shape=[jax.ShapeDtypeStruct((r, HEADS * HEAD_SIZE), jnp.bfloat16) for r in rows],
        in_specs=[whole(pltpu.SMEM)] * scalars + [whole()] * (len(arrays) - scalars),
        out_specs=[whole()] * len(rows),
        compiler_params=SMALL,
        name="unpack",
    )(*arrays)


def merge(groups, *arrays):
    return pl.pallas_call(
        functools.partial(merge_kernel, groups - 1),
        out_shape=[BLOCK_KV] * MEMBERS,
        in_specs=[whole(pltpu.SMEM)] * 2 + [whole()] * 5,
        out_specs=[whole()] * MEMBERS,
        scratch_shapes=[pltpu.VMEM((MEMBERS, ROWS, GROUP_WIDTH), jnp.bfloat16)],
        compiler_params=SMALL,
        name="merge",
    )(*arrays)


def attention(groups, group, *arrays):
    def head_block(*leading):
        zeros = (0,) * len(leading)
        return pl.BlockSpec(leading + (HEAD_SIZE,), lambda head: zeros + (head,))

    return pl.pallas_call(
        functools.partial(attention_kernel, groups - 1),
        grid=(GROUP_HEADS,),
        out_shape=[PACKED_KV] * 2 + [BLOCK_KV] * 3,
        in_specs=[
            whole(pltpu.SMEM),
            whole(pltpu.SMEM),
            head_block(MEMBERS, ROWS),
            head_block(MEMBERS, ROWS),
            *[head_block(ROWS)] * 4,
        ],
        out_specs=[head_block(MEMBERS, ROWS)] * 2 + [head_block(ROWS)] * 3,
        scratch_shapes=[pltpu.VMEM((ROWS, HEAD_SIZE), jnp.bfloat16)],
        compiler_params=LARGE,
        name="attention",
    )(group, *arrays)


def slice_shift():
    clip, tower = lax.axis_index("clip"), lax.axis_index("tower")
    shifted = (clip == lax.axis_size("clip") - 1) & (tower == 1)
    return jnp.where(shifted, 1, 0).astype(jnp.int32).reshape(1)


def moved(block, hops):
    clips, towers = lax.axis_size("clip"), lax.axis_size("tower")
    per_tower = lax.axis_size("group")
    route = []
    for clip in range(clips):
        for group, target in hops:
            turn = target // per_tower - group // per_tower if clip == clips - 1 else 0
            for member in range(MEMBERS):
                route.append(
                    (
                        (clip * towers * per_tower + group) * MEMBERS + member,
                        (clip * towers * per_tower + target) * MEMBERS
                        + (member - turn) % MEMBERS,
                    )
                )
    return lax.ppermute(block, ("clip", "tower", "group", "member"), route)


def to_group(block, distance):
    groups = lax.axis_size(("tower", "group"))
    hops = [(g, g + distance) for g in range(groups) if 0 <= g + distance < groups]
    return moved(block, hops)


def to_group_by_relay(block, distance):
    groups, per_tower = lax.axis_size(("tower", "group")), lax.axis_size("group")
    relay = 0 if distance > 0 else groups - 1
    first, second = [], []
    for group in range(groups):
        target = group + distance
        if not 0 <= target < groups:
            continue
        if group // per_tower == target // per_tower:
            first.append((group, target))
        else:
            first.append((group, relay))
            second.append((relay, target))
    arrived = moved(block, first)
    return arrived, moved(arrived, second)


def exchange(packed):
    return lax.all_to_all(packed, "member", 0, 0)


def send_round(blocks):
    received = {0: blocks[0]}
    for d in range(1, MEMBERS):
        route = [(i, (i + d) % MEMBERS) for i in range(MEMBERS)]
        received[d] = lax.ppermute(blocks[d], "member", route)
    return [received[d] for d in DISTANCES]


def body(
    video_query,
    video_keys,
    video_value,
    audio_query,
    audio_key,
    audio_value,
    video_cotangent,
    audio_cotangent,
    video_lists,
    audio_lists,
):
    groups = lax.axis_size(("tower", "group"))
    group = lax.axis_index(("tower", "group")).astype(jnp.int32).reshape(1)
    shift = slice_shift()
    me = lax.axis_index("member").astype(jnp.int32).reshape(1)
    kv_packed = pack_kv(shift, video_keys, video_value, audio_key, audio_value)
    kv = exchange(kv_packed)
    qg_packed = pack_qg(
        shift,
        video_query,
        audio_query,
        video_cotangent,
        audio_cotangent,
    )
    before_3, relayed_3 = to_group_by_relay(kv[3], 1)
    before_2 = to_group(kv[2], 1)
    after = to_group(kv[0], -1)
    qg = exchange(qg_packed)
    own_firsts = jnp.concatenate([video_lists[:, :1], audio_lists[:, :1]], axis=1)
    firsts = lax.all_gather(own_firsts, "member", axis=0, tiled=True)
    qg_part, kv_part, part_2, part_3, after_part = attention(
        groups, group, firsts, kv, qg, before_2, before_3, relayed_3, after
    )
    qg_back = exchange(qg_part)
    from_after_3, relayed_back = to_group_by_relay(part_3, -1)
    from_after_2 = to_group(part_2, -1)
    from_before = to_group(after_part, 1)
    kvs_back = send_round(
        merge(
            groups,
            group,
            me,
            kv_part,
            from_after_2,
            from_after_3,
            relayed_back,
            from_before,
        )
    )
    video_output, audio_output, video_query_grad, audio_query_grad = unpack(
        unpack_qg_kernel, (VIDEO, AUDIO, VIDEO, AUDIO), shift, qg_back
    )
    video_key_grad, video_value_grad, audio_key_grad, audio_value_grad = unpack(
        unpack_kv_kernel, (VIDEO, VIDEO, AUDIO, AUDIO), shift, me, *kvs_back
    )
    return (
        video_output,
        audio_output,
        video_query_grad,
        video_key_grad,
        video_value_grad,
        audio_query_grad,
        audio_key_grad,
        audio_value_grad,
    )


def solution(mesh):
    shape = mesh.devices.shape
    fine = Mesh(
        mesh.devices.reshape(shape[0], shape[1], shape[2] // MEMBERS, MEMBERS),
        ("clip", "tower", "group", "member"),
    )
    placed = P(("clip", "tower", "group", "member"), None)
    return jax.shard_map(
        body,
        mesh=fine,
        in_specs=(placed,) * 10,
        out_specs=(placed,) * 8,
        check_vma=False,
    )
```
